512 devices in a mesh: dp: 64 (over z, y_hi, core), blk: 8 (over x, y_lo).
Axes of the slice: x: 4, y: 8 (y_hi: 4, y_lo: 2; y = y_hi * 2 + y_lo), z: 8, core: 2. Of those that a mesh axis runs over, the one named last changes fastest.
Arguments:
- activations: bfloat16 [40960, 3584], P('dp'), may hold values from -16 to 16
Outputs:
- factor_blocks: float32 [512, 16384], P('dp', 'blk')
The draws below stay inside these ranges and needn't reach their ends.
All inputs are finite; a program needn't handle non-finite values.
Results may differ from the reference program's by a relative error of at most 0.0003.
Values sent between devices are 32-bit elements; how exact they have to be, the bound alone decides.
No kernel may reach another device: no remote copies, remote signals or barrier semaphores. Data moves between devices by JAX's collectives and lax.ppermute only.
A program may use at most 64 MiB of HBM per device.

```python
import jax
import jax.numpy as jnp
from jax import lax

M = 3584
BS = 512
TOKENS = 40960
N_BLK = 8


def spiked(entries, key, source, target, shards_of, factor):
    def block_of(axis_at):
        return (jnp.arange(entries.shape[axis_at]) // (entries.shape[axis_at] // shards_of)).reshape((-1,) + (1,) * (entries.ndim - 1 - axis_at))

    one_side = jax.random.permutation(key, shards_of)[block_of(target)]
    second = (block_of(target) + shards_of // 2) % shards_of
    return jnp.where((block_of(source) == one_side) | (block_of(source) == second), factor * entries, entries)


def steps_of(rng, dims, pieces, low, high):
    def one(position, parts):
        heights = jax.random.uniform(jax.random.fold_in(jax.random.fold_in(rng, 6), position), (parts,), jnp.float32, low / len(pieces), high / len(pieces))
        return jnp.repeat(jnp.exp(heights), dims[position] // parts).reshape((-1,) + (1,) * (len(dims) - position - 1))

    factor_of = one(*pieces[0])
    for cut in pieces[1:]:
        factor_of = factor_of * one(*cut)
    return factor_of


def gaussian_with(key, shape, spread, bound, shards, heavy, kind=jnp.bfloat16):
    drawn = spread * jax.random.normal(key, shape, jnp.float32)
    if shards:
        drawn = drawn * steps_of(key, shape, shards, -0.22, 0.18)
    return jnp.clip(spiked(drawn, jax.random.fold_in(key, 3), *heavy), -bound, bound).astype(kind)


def setup_inputs(seed: int = 0) -> dict:
    arg_keys = jax.random.split(jax.random.key(seed), 2)
    activations = gaussian_with(arg_keys[0], (TOKENS, M), 1.0, 16.0, ((0, 64),), (0, 1, 64, 4.0))
    return dict(activations=activations)


DAMPING = 0.1

def block_pairs(count):
    return [(i, j) for j in range(count) for i in range(j, count)]

def reference(activations):
    widened = activations.astype(jnp.float32)
    factor = jnp.dot(widened.T, widened, precision=lax.Precision.HIGHEST) / TOKENS
    factor = factor + DAMPING * jnp.eye(M, dtype=jnp.float32)
    corner = jnp.linalg.cholesky(factor[:BS, :BS])
    identity = jnp.eye(BS, dtype=jnp.float32)
    corner_inverse = lax.linalg.triangular_solve(corner, identity, left_side=True, lower=True)
    solved = jnp.dot(factor[:, :BS], corner_inverse.T, precision=lax.Precision.HIGHEST)
    panel = jnp.concatenate([corner, solved[BS:]], axis=0)
    lower_panel = panel[BS:]
    trailing = factor[BS:, BS:] - jnp.dot(lower_panel, lower_panel.T, precision=lax.Precision.HIGHEST)
    pair_list = block_pairs(M // BS)
    slot_count = (len(pair_list) + N_BLK - 1) // N_BLK
    columns = []
    for owner in range(N_BLK):
        for slot in range(slot_count):
            index = slot * N_BLK + owner
            if index < len(pair_list):
                i, j = pair_list[index]
                if j == 0:
                    columns.append(panel[i * BS:(i + 1) * BS])
                else:
                    columns.append(trailing[(i - 1) * BS:i * BS, (j - 1) * BS:j * BS])
            else:
                columns.append(jnp.zeros((BS, BS), jnp.float32))
    return jnp.concatenate(columns, axis=1)
```

```python
import jax
import jax.numpy as jnp
import numpy as np
from jax import lax
from jax.experimental import pallas as pl
from jax.experimental.pallas import tpu as pltpu
from jax.sharding import PartitionSpec as P

BS = 512
HALF = 256
NB = 128
NZ, NY, NC, NBLK = 8, 4, 2, 8
TOKENS = 40960
DAMPING = 0.1
F32 = jnp.float32
VMEM_LIMIT = 40 * 1024 * 1024
GRAM_LIMIT = 60 * 1024 * 1024
CORNER_FLOPS = 20_000_000_000

HELD = (2, 1, 2, 3, 4, 5, 6, 1)
TRAIL = (
    ((6, 4), (2, 1), (5, 2)),
    ((5, 5), (6, 2), (3, 1)),
    ((3, 3), (6, 5), (4, 1)),
    ((6, 6), (5, 1), (4, 3)),
    ((6, 1), (5, 3), None),
    ((2, 2), None, (6, 3)),
    (None, (4, 4), (3, 2)),
    ((4, 2), (1, 1), (5, 4)),
)
ROUNDS = (
    ((3, 2), (4, 0), (5, 1), (6, 3), (7, 4), (2, 5), (0, 7)),
    ((3, 4), (4, 6), (5, 2), (1, 0), (7, 3), (0, 1)),
    ((3, 5), (4, 7), (1, 2), (2, 6)),
)


def owner_tables():
    count = BS * 7 // BS
    order = [(i, j) for j in range(count) for i in range(j, count)]
    slot_of = {pair: (t % NBLK, t // NBLK) for t, pair in enumerate(order)}
    rows = []
    for owner in range(NBLK):
        row = [HELD[owner], owner if 0 < owner < 7 else 1]
        for r in range(3):
            pair = TRAIL[owner][r]
            if pair is None:
                row += [1, 1, 0, 0, 0]
                continue
            at, slot = slot_of[pair]
            assert at == owner
            sent = [s for s, d in ROUNDS[r] if d == owner]
            own = 0 if sent else 1
            assert HELD[sent[0] if sent else owner] == pair[1]
            row += [pair[0], pair[1], 1, own, slot]
        rows.append(row)
    return np.asarray(rows, np.int32)


CORE, RANK, OWNER, HELD_AT, CORNER, ROW_I, COL_J, LIVE, OWN, SLOT, PANEL_SLOT = 0, 1, 2, 3, 4, 5, 9, 12, 15, 18, 21
WIDTH = 24


def device_table():
    per_owner = owner_tables()
    table = np.zeros((NZ * NY * NC * NBLK, WIDTH), np.int32)
    for group in range(NZ * NY * NC):
        for owner in range(NBLK):
            row = table[group * NBLK + owner]
            mine = per_owner[owner]
            row[CORE], row[RANK], row[OWNER] = group % NC, group // NC, owner
            row[HELD_AT], row[CORNER] = mine[0], owner == 0
            row[ROW_I] = mine[1]
            for e in range(3):
                i, j, live, own, slot = mine[2 + 5 * e : 7 + 5 * e]
                row[ROW_I + 1 + e], row[COL_J + e], row[LIVE + e], row[OWN + e], row[SLOT + e] = i, j, live, own, slot
            row[PANEL_SLOT] = 0 if owner < 7 else -1
    return table


def split(x):
    hi = x.astype(jnp.bfloat16)
    return hi, (x - hi.astype(F32)).astype(jnp.bfloat16)


def dot3(a, b, dims):
    def one(u, v):
        return lax.dot_general(u, v, (dims, ((), ())), preferred_element_type=F32)

    return one(a[0], b[0]) + (one(a[0], b[1]) + one(a[1], b[0]))


NT = ((1,), (1,))
NN = ((1,), (0,))
TN = ((0,), (0,))


def gram(a, b):
    return lax.dot_general(a, b, (TN, ((), ())), preferred_element_type=F32)


def first_column_kernel(s_ref, a0_ref, ai_ref, mine_ref, other_ref, d_ref):
    core = s_ref[CORE]
    owner = s_ref[OWNER]
    a0 = a0_ref[...]
    d_ref[...] = gram(a0, a0)
    for half in range(NC):
        block = gram(ai_ref[...], a0[:, half * HALF : (half + 1) * HALF])

        def store(out_ref):
            for z in range(NZ):
                row = pl.multiple_of(owner * 64 + z * 8, 8)
                out_ref[z, 0:8, :] = d_ref[pl.ds(row, 8), half * HALF : (half + 1) * HALF]
                out_ref[z, 8:72, :] = block[z * 64 : (z + 1) * 64, :]

        @pl.when(core == half)
        def _():
            store(mine_ref)

        @pl.when(core != half)
        def _():
            store(other_ref)


def sum_z_kernel(x_ref, after_ref, out_ref):
    del after_ref
    total = x_ref[0]
    for z in range(1, NZ):
        total = total + x_ref[z]
    for y in range(NY):
        out_ref[y] = total


def sum_y_kernel(s_ref, x_ref, after_ref, corner_ref, held_ref, rows_ref):
    del after_ref
    total = x_ref[0]
    for y in range(1, NY):
        total = total + x_ref[y]
    for z in range(NZ):
        corner_ref[z] = total[0:8, :]
        held_ref[z] = total[8:72, :]
    for y in range(NY):

        @pl.when(lax.rem(s_ref[RANK], NY) == y)
        def _():
            rows_ref[...] = total[8 + 16 * y : 24 + 16 * y, :]


HBM = pl.BlockSpec(memory_space=pltpu.HBM)


def trailing_kernel(s_ref, ai_ref, aj_ref, after_ref, mine_ref, other_ref):
    del after_ref
    core = s_ref[CORE]
    block = gram(ai_ref[...], aj_ref[...])
    for half in range(NC):

        def store(out_ref):
            for q in range(NZ * NY):
                out_ref[8 * q : 8 * q + 8, :] = block[16 * q + 8 * half : 16 * q + 8 * half + 8, :]

        @pl.when(core == half)
        def _():
            store(mine_ref)

        @pl.when(core != half)
        def _():
            store(other_ref)


def eliminate(T):
    n = len(T)
    T = list(T)
    lane = lax.broadcasted_iota(jnp.int32, (8, NB), 1)
    sub = lax.broadcasted_iota(jnp.int32, (8, NB), 0)
    out = [None] * n
    for g in range(n):
        c0 = 8 * g
        V = [jnp.broadcast_to(T[g][:, c0 + k : c0 + k + 1], (8, NB)) for k in range(8)]
        ingroup = (lane >= c0) & (lane < c0 + 8)
        R = jnp.where(ingroup, jnp.where(lane == sub + c0, 1.0, 0.0), T[g])
        rcp, d, rows = [], [], []
        pivot = jnp.ones((8, NB), F32)
        for k in range(8):
            dk = [jnp.broadcast_to(V[j][k : k + 1, :], (8, NB)) for j in range(k, 8)]
            r = 1.0 / dk[0]
            pivot = jnp.where(sub == k, dk[0], pivot)
            Rk = jnp.broadcast_to(R[k : k + 1, :], (8, NB))
            rcp.append(r)
            d.append(dk)
            rows.append(Rk)
            if k < 7:
                m = jnp.where(sub > k, V[k] * r, 0.0)
                for j in range(k + 1, 8):
                    V[j] = V[j] - m * dk[j - k]
                R = R - m * Rk
        out[g] = jnp.where(lane < c0 + 8, R * lax.rsqrt(pivot), 0.0)
        for s in range(g + 1, n):
            V = [jnp.broadcast_to(T[s][:, c0 + k : c0 + k + 1], (8, NB)) for k in range(8)]
            R = jnp.where(ingroup, 0.0, T[s])
            for k in range(8):
                m = V[k] * rcp[k]
                for j in range(k + 1, 8):
                    V[j] = V[j] - m * d[k][j - k]
                R = R - m * rows[k]
            T[s] = R
    return out


def corner_kernel(s_ref, mine_ref, other_ref, p_ref, w_ref, a_ref, c_ref, i_ref, x_ref, px_ref):
    core = s_ref[CORE]
    rank = s_ref[RANK]
    is_corner = s_ref[CORNER]
    n = BS // NB
    scale = 1.0 / TOKENS
    for half in range(NC):
        cols = slice(half * HALF, (half + 1) * HALF)

        def load(src_ref):
            for o in range(NBLK):
                a_ref[64 * o : 64 * o + 64, cols] = src_ref[o, 0:64, :] * scale
            for q in range(4):
                x_ref[16 * q : 16 * q + 16, cols] = src_ref[s_ref[ROW_I + q], 64:80, :] * scale

        @pl.when(core == half)
        def _():
            load(mine_ref)

        @pl.when(core != half)
        def _():
            load(other_ref)

    row = lax.broadcasted_iota(jnp.int32, (NB, NB), 0)
    col = lax.broadcasted_iota(jnp.int32, (NB, NB), 1)
    for b in range(n):
        at = slice(b * NB, (b + 1) * NB)
        a_ref[at, at] = a_ref[at, at] + jnp.where(row == col, DAMPING, 0.0)

    @pl.when(is_corner == 1)
    def _():
        x_ref[0:16, :] = a_ref[pl.ds(pl.multiple_of(rank * 16, 16), 16), :]

    for b in range(n):
        o = b * NB
        out = eliminate([a_ref[o + 8 * g : o + 8 * g + 8, o : o + NB] for g in range(NB // 8)])
        for g in range(NB // 8):
            i_ref[b, 8 * g : 8 * g + 8, :] = out[g]
        inv = split(i_ref[b])
        xf = dot3(split(x_ref[:, o : o + NB]), inv, NT)
        px_ref[:, o : o + NB] = xf
        if b < n - 1:
            X = dot3(split(a_ref[o + NB :, o : o + NB]), inv, NT)
            c_ref[o + NB :, o : o + NB] = X
            Xs = split(X)
            a_ref[o + NB :, o + NB :] = a_ref[o + NB :, o + NB :] - dot3(Xs, Xs, NT)
            x_ref[:, o + NB :] = x_ref[:, o + NB :] - dot3(split(xf), Xs, NT)
    panel = px_ref[0:16, :]
    grow = rank * 16 + lax.broadcasted_iota(jnp.int32, (16, BS), 0)
    gcol = lax.broadcasted_iota(jnp.int32, (16, BS), 1)
    panel = jnp.where((is_corner == 1) & (gcol > grow), 0.0, panel)
    p_ref[...] = panel
    ws = [None] * n
    wv = [None] * n
    for b in reversed(range(n)):
        o = b * NB
        acc = px_ref[16:, o : o + NB]
        for i in range(b + 1, n):
            acc = acc - dot3(ws[i], split(c_ref[i * NB : (i + 1) * NB, o : o + NB]), NN)
        wv[b] = dot3(split(acc), split(i_ref[b]), NN)
        ws[b] = split(wv[b])
    for half in range(NC):

        @pl.when(core == half)
        def _():
            for q in range(2):
                w_ref[:, q * NB : (q + 1) * NB] = wv[2 * half + q]


def update_kernel(s_ref, w_ref, own_ref, r0_ref, r1_ref, r2_ref, mine_ref, other_ref):
    core = s_ref[CORE]
    for e, recv_ref in enumerate((r0_ref, r1_ref, r2_ref)):
        own = s_ref[OWN + e]
        got = jnp.where(own == 1, own_ref[...], recv_ref[...])
        part = dot3(split(w_ref[16 * e : 16 * e + 16, :]), split(got), NT)
        cols = slice(e * BS, (e + 1) * BS)
        low, high = part[0:8, :], part[8:16, :]
        mine_ref[:, cols] = jnp.where(core == 0, low, high)
        other_ref[:, cols] = jnp.where(core == 0, high, low)


def finish_kernel(s_ref, panel_ref, rest_ref, mine_ref, other_ref, out_ref):
    core = s_ref[CORE]
    row = s_ref[RANK] * 16 + core * 8 + lax.broadcasted_iota(jnp.int32, (8, BS), 0)
    col = lax.broadcasted_iota(jnp.int32, (8, BS), 1)
    panel = jnp.where(core == 0, panel_ref[0:8, :], panel_ref[8:16, :])
    values = []
    for e in range(3):
        cols = slice(e * BS, (e + 1) * BS)
        value = (rest_ref[:, cols] - (mine_ref[:, cols] + other_ref[:, cols])) * (1.0 / TOKENS)
        on_diagonal = s_ref[ROW_I + 1 + e] == s_ref[COL_J + e]
        values.append(value + jnp.where(on_diagonal & (row == col), DAMPING, 0.0))
    for slot in range(4):
        out = jnp.where(s_ref[PANEL_SLOT] == slot, panel, 0.0)
        for e in range(3):
            out = jnp.where((s_ref[SLOT + e] == slot) & (s_ref[LIVE + e] == 1), values[e], out)
        out_ref[:, slot * BS : (slot + 1) * BS] = out


def vmem(count):
    return [pl.BlockSpec(memory_space=pltpu.VMEM)] * count


SMEM = pl.BlockSpec(memory_space=pltpu.SMEM)


def params(limit=VMEM_LIMIT):
    return pltpu.CompilerParams(vmem_limit_bytes=limit)


def dp_index(z, y, c):
    return (z * NY + y) * NC + c


Z_GROUPS = [[dp_index(z, y, c) for z in range(NZ)] for y in range(NY) for c in range(NC)]
Y_GROUPS = [[dp_index(z, y, c) for y in range(NY)] for z in range(NZ) for c in range(NC)]
CORE_SWAP = [(dp_index(z, y, c), dp_index(z, y, 1 - c)) for z in range(NZ) for y in range(NY) for c in range(NC)]


def exchange(x, groups):
    return lax.all_to_all(x, "dp", 0, 0, axis_index_groups=groups)


def body(act):
    tok = act.shape[0]
    group = lax.axis_index("dp")
    place = lax.dynamic_index_in_dim(
        jnp.asarray(device_table()), group * NBLK + lax.axis_index("blk"), 0, keepdims=False
    )

    piece = jax.ShapeDtypeStruct((NZ, 72, HALF), F32)
    mine, other = pl.pallas_call(
        first_column_kernel,
        out_shape=[piece, piece],
        grid_spec=pltpu.PrefetchScalarGridSpec(
            num_scalar_prefetch=1,
            grid=(1,),
            in_specs=[
                pl.BlockSpec((tok, BS), lambda g, s: (0, 0)),
                pl.BlockSpec((tok, BS), lambda g, s: (0, s[HELD_AT])),
            ],
            out_specs=[pl.BlockSpec((NZ, 72, HALF), lambda g, s: (0, 0, 0))] * 2,
            scratch_shapes=[pltpu.VMEM((BS, BS), F32)],
        ),
        compiler_params=params(GRAM_LIMIT),
        name="first_column",
    )(place, act, act)
    first = mine + lax.ppermute(other, "dp", CORE_SWAP)
    over_z = exchange(first, Z_GROUPS)

    wide = jax.ShapeDtypeStruct((BS // 2, 3 * BS), F32)
    mine, other = pl.pallas_call(
        trailing_kernel,
        out_shape=[wide, wide],
        grid_spec=pltpu.PrefetchScalarGridSpec(
            num_scalar_prefetch=1,
            grid=(3,),
            in_specs=[
                pl.BlockSpec((tok, BS), lambda e, s: (0, s[ROW_I + 1 + e])),
                pl.BlockSpec((tok, BS), lambda e, s: (0, s[COL_J + e])),
                HBM,
            ],
            out_specs=[pl.BlockSpec((BS // 2, BS), lambda e, s: (0, e))] * 2,
        ),
        compiler_params=params(GRAM_LIMIT),
        cost_estimate=pl.CostEstimate(flops=4_000_000_000, bytes_accessed=7_000_000, transcendentals=0),
        name="trailing_gram",
    )(place, act, act, first)
    both = mine + lax.ppermute(other, "dp", CORE_SWAP)
    rest = lax.psum_scatter(both, "dp", scatter_dimension=0, tiled=True, axis_index_groups=Z_GROUPS)
    rest = lax.psum_scatter(rest, "dp", scatter_dimension=0, tiled=True, axis_index_groups=Y_GROUPS)

    spread = pl.pallas_call(
        sum_z_kernel,
        out_shape=jax.ShapeDtypeStruct((NY, 72, HALF), F32),
        in_specs=vmem(1) + [HBM],
        out_specs=vmem(1)[0],
        name="sum_over_z",
    )(over_z, other)
    over_y = exchange(spread, Y_GROUPS)
    corner_rows, held_rows, own_rows = pl.pallas_call(
        sum_y_kernel,
        out_shape=[
            jax.ShapeDtypeStruct((NZ, 8, HALF), F32),
            jax.ShapeDtypeStruct((NZ, 64, HALF), F32),
            jax.ShapeDtypeStruct((16, HALF), F32),
        ],
        in_specs=[SMEM] + vmem(1) + [HBM],
        out_specs=vmem(3),
        name="sum_over_y",
    )(place, over_y, both)

    corner_rows = exchange(corner_rows, Z_GROUPS)
    column = exchange(held_rows, Z_GROUPS).reshape(BS, HALF)
    share = jnp.concatenate([corner_rows.reshape(64, HALF), own_rows], axis=0)
    share = lax.all_to_all(jnp.broadcast_to(share, (NBLK, 80, HALF)), "blk", 0, 0)
    share_other = lax.ppermute(share, "dp", CORE_SWAP)
    brought = [lax.ppermute(column, "blk", list(pairs)) for pairs in ROUNDS]

    panel, w = pl.pallas_call(
        corner_kernel,
        out_shape=[jax.ShapeDtypeStruct((16, BS), F32), jax.ShapeDtypeStruct((48, HALF), F32)],
        in_specs=[SMEM] + vmem(2),
        out_specs=vmem(2),
        scratch_shapes=[
            pltpu.VMEM((BS, BS), F32),
            pltpu.VMEM((BS, BS), F32),
            pltpu.VMEM((BS // NB, NB, NB), F32),
            pltpu.VMEM((64, BS), F32),
            pltpu.VMEM((64, BS), F32),
        ],
        compiler_params=params(),
        cost_estimate=pl.CostEstimate(flops=CORNER_FLOPS, bytes_accessed=2_000_000, transcendentals=0),
        name="corner",
    )(place, share, share_other)

    part = jax.ShapeDtypeStruct((8, 3 * BS), F32)
    mine, other = pl.pallas_call(
        update_kernel,
        out_shape=[part, part],
        in_specs=[SMEM] + vmem(5),
        out_specs=vmem(2),
        compiler_params=params(),
        name="update",
    )(place, w, column, *brought)
    return pl.pallas_call(
        finish_kernel,
        out_shape=jax.ShapeDtypeStruct((8, 4 * BS), F32),
        in_specs=[SMEM] + vmem(4),
        out_specs=vmem(1)[0],
        name="finish",
    )(place, panel, rest, mine, lax.ppermute(other, "dp", CORE_SWAP))


def solution(mesh):
    return jax.shard_map(body, mesh=mesh, in_specs=(P("dp", None),), out_specs=P("dp", "blk"), check_vma=False)
```

```python
import jax
import jax.numpy as jnp
import numpy as np
from jax import lax
from jax.experimental import pallas as pl
from jax.experimental.pallas import tpu as pltpu
from jax.sharding import PartitionSpec as P

BS = 512
HALF = 256
NB = 128
NZ, NY, NC, NBLK = 8, 4, 2, 8
TOKENS = 40960
DAMPING = 0.1
F32 = jnp.float32
VMEM_LIMIT = 40 * 1024 * 1024
GRAM_LIMIT = 60 * 1024 * 1024
CORNER_FLOPS = 20_000_000_000

HELD = (2, 1, 2, 3, 4, 5, 6, 1)
TRAIL = (
    ((6, 4), (2, 1), (5, 2)),
    ((5, 5), (6, 2), (3, 1)),
    ((3, 3), (6, 5), (4, 1)),
    ((6, 6), (5, 1), (4, 3)),
    ((6, 1), (5, 3), None),
    ((2, 2), None, (6, 3)),
    (None, (4, 4), (3, 2)),
    ((4, 2), (1, 1), (5, 4)),
)
ROUNDS = (
    ((3, 2), (4, 0), (5, 1), (6, 3), (7, 4), (2, 5), (0, 7)),
    ((3, 4), (4, 6), (5, 2), (1, 0), (7, 3), (0, 1)),
    ((3, 5), (4, 7), (1, 2), (2, 6)),
)


def owner_tables():
    count = BS * 7 // BS
    order = [(i, j) for j in range(count) for i in range(j, count)]
    slot_of = {pair: (t % NBLK, t // NBLK) for t, pair in enumerate(order)}
    rows = []
    for owner in range(NBLK):
        row = [HELD[owner], owner if 0 < owner < 7 else 1]
        for r in range(3):
            pair = TRAIL[owner][r]
            if pair is None:
                row += [1, 1, 0, 0, 0]
                continue
            at, slot = slot_of[pair]
            assert at == owner
            sent = [s for s, d in ROUNDS[r] if d == owner]
            own = 0 if sent else 1
            assert HELD[sent[0] if sent else owner] == pair[1]
            row += [pair[0], pair[1], 1, own, slot]
        rows.append(row)
    return np.asarray(rows, np.int32)


CORE, RANK, OWNER, HELD_AT, CORNER, ROW_I, COL_J, LIVE, OWN, SLOT, PANEL_SLOT = 0, 1, 2, 3, 4, 5, 9, 12, 15, 18, 21
WIDTH = 24


def device_table():
    per_owner = owner_tables()
    table = np.zeros((NZ * NY * NC * NBLK, WIDTH), np.int32)
    for group in range(NZ * NY * NC):
        for owner in range(NBLK):
            row = table[group * NBLK + owner]
            mine = per_owner[owner]
            row[CORE], row[RANK], row[OWNER] = group % NC, group // NC, owner
            row[HELD_AT], row[CORNER] = mine[0], owner == 0
            row[ROW_I] = mine[1]
            for e in range(3):
                i, j, live, own, slot = mine[2 + 5 * e : 7 + 5 * e]
                row[ROW_I + 1 + e], row[COL_J + e], row[LIVE + e], row[OWN + e], row[SLOT + e] = i, j, live, own, slot
            row[PANEL_SLOT] = 0 if owner < 7 else -1
    return table


def split(x):
    hi = x.astype(jnp.bfloat16)
    return hi, (x - hi.astype(F32)).astype(jnp.bfloat16)


def dot3(a, b, dims):
    def one(u, v):
        return lax.dot_general(u, v, (dims, ((), ())), preferred_element_type=F32)

    return one(a[0], b[0]) + (one(a[0], b[1]) + one(a[1], b[0]))


NT = ((1,), (1,))
NN = ((1,), (0,))
TN = ((0,), (0,))


def gram(a, b):
    return lax.dot_general(a, b, (TN, ((), ())), preferred_element_type=F32)


def first_column_kernel(s_ref, a0_ref, ai_ref, mine_ref, other_ref, d_ref):
    core = s_ref[CORE]
    owner = s_ref[OWNER]
    a0 = a0_ref[...]
    d_ref[...] = gram(a0, a0)
    for half in range(NC):
        block = gram(ai_ref[...], a0[:, half * HALF : (half + 1) * HALF])

        def store(out_ref):
            for z in range(NZ):
                row = pl.multiple_of(owner * 64 + z * 8, 8)
                out_ref[z, 0:8, :] = d_ref[pl.ds(row, 8), half * HALF : (half + 1) * HALF]
                out_ref[z, 8:72, :] = block[z * 64 : (z + 1) * 64, :]

        @pl.when(core == half)
        def _():
            store(mine_ref)

        @pl.when(core != half)
        def _():
            store(other_ref)


def sum_z_kernel(x_ref, out_ref):
    total = x_ref[0]
    for z in range(1, NZ):
        total = total + x_ref[z]
    for y in range(NY):
        out_ref[y] = total


def sum_y_kernel(s_ref, x_ref, corner_ref, held_ref, rows_ref):
    total = x_ref[0]
    for y in range(1, NY):
        total = total + x_ref[y]
    for z in range(NZ):
        corner_ref[z] = total[0:8, :]
        held_ref[z] = total[8:72, :]
    for y in range(NY):

        @pl.when(lax.rem(s_ref[RANK], NY) == y)
        def _():
            rows_ref[...] = total[8 + 16 * y : 24 + 16 * y, :]


def pass_kernel(x_ref, after_ref, out_ref):
    del x_ref, after_ref, out_ref


HBM = pl.BlockSpec(memory_space=pltpu.HBM)


def after(x, dep):
    return pl.pallas_call(
        pass_kernel,
        out_shape=jax.ShapeDtypeStruct(x.shape, x.dtype),
        in_specs=[HBM, HBM],
        out_specs=HBM,
        input_output_aliases={0: 0},
        name="after",
    )(x, dep)


def trailing_kernel(s_ref, ai_ref, aj_ref, after_ref, out_ref):
    del s_ref, after_ref
    out_ref[...] = gram(ai_ref[...], aj_ref[...])


def recip(x):
    r = pl.reciprocal(x, approx=True)
    return r * (2.0 - x * r)


def lanes(x, c):
    return jnp.broadcast_to(x[:, c : c + 1], (8, NB))


def sublanes(x, k):
    return jnp.broadcast_to(x[k : k + 1, :], (8, NB))


def eliminate(T):
    n = len(T)
    T = list(T)
    lane = lax.broadcasted_iota(jnp.int32, (8, NB), 1)
    sub = lax.broadcasted_iota(jnp.int32, (8, NB), 0)
    out = [None] * n
    own = [lanes(T[0], k) for k in range(8)]
    for g in range(n):
        c0 = 8 * g
        last = g == n - 1
        V = list(own) + ([] if last else [lanes(T[g], c0 + 8 + k) for k in range(8)])
        if not last:
            A = [lanes(T[g + 1], c0 + k) for k in range(8)]
            U = [lanes(T[g + 1], c0 + 8 + k) for k in range(8)]
        ingroup = (lane >= c0) & (lane < c0 + 8)
        R = jnp.where(ingroup, jnp.where(lane == sub + c0, 1.0, 0.0), T[g])
        R1 = None if last else jnp.where(ingroup, 0.0, T[g + 1])
        rcp, d, rows = [], [], []
        pivot = jnp.ones((8, NB), F32)
        for k in range(8):
            dk = [sublanes(V[j], k) for j in range(k, len(V))]
            r = recip(dk[0])
            pivot = jnp.where(sub == k, dk[0], pivot)
            Rk = sublanes(R, k)
            rcp.append(r)
            d.append(dk)
            rows.append(Rk)
            if k < 7:
                m = jnp.where(sub > k, V[k], 0.0) * r
                for j in range(k + 1, len(V)):
                    V[j] = V[j] - m * dk[j - k]
                R = R - m * Rk
            if not last:
                m = A[k] * r
                for j in range(k + 1, 8):
                    A[j] = A[j] - m * dk[j - k]
                for j in range(8):
                    U[j] = U[j] - m * dk[8 + j - k]
                R1 = R1 - m * Rk
        out[g] = jnp.where(lane < c0 + 8, R * lax.rsqrt(pivot), 0.0)
        if not last:
            T[g + 1] = R1
            own = U
        for s in range(g + 2, n):
            W = [lanes(T[s], c0 + k) for k in range(8)]
            R = jnp.where(ingroup, 0.0, T[s])
            for k in range(8):
                m = W[k] * rcp[k]
                for j in range(k + 1, 8):
                    W[j] = W[j] - m * d[k][j - k]
                R = R - m * rows[k]
            T[s] = R
    return out


def corner_kernel(s_ref, mine_ref, other_ref, p_ref, w_ref, a_ref, c_ref, i_ref, x_ref, px_ref):
    core = s_ref[CORE]
    rank = s_ref[RANK]
    is_corner = s_ref[CORNER]
    n = BS // NB
    scale = 1.0 / TOKENS
    for half in range(NC):
        cols = slice(half * HALF, (half + 1) * HALF)

        def load(src_ref):
            for o in range(NBLK):
                a_ref[64 * o : 64 * o + 64, cols] = src_ref[o, 0:64, :] * scale
            for q in range(4):
                x_ref[16 * q : 16 * q + 16, cols] = src_ref[s_ref[ROW_I + q], 64:80, :] * scale

        @pl.when(core == half)
        def _():
            load(mine_ref)

        @pl.when(core != half)
        def _():
            load(other_ref)

    row = lax.broadcasted_iota(jnp.int32, (NB, NB), 0)
    col = lax.broadcasted_iota(jnp.int32, (NB, NB), 1)
    for b in range(n):
        at = slice(b * NB, (b + 1) * NB)
        a_ref[at, at] = a_ref[at, at] + jnp.where(row == col, DAMPING, 0.0)

    @pl.when(is_corner == 1)
    def _():
        x_ref[0:16, :] = a_ref[pl.ds(pl.multiple_of(rank * 16, 16), 16), :]

    def rest_of(b, o, inv):
        xf = dot3(split(x_ref[:, o : o + NB]), inv, NT)
        px_ref[:, o : o + NB] = xf
        if b == n - 1:
            return
        near, far = slice(o + NB, o + 2 * NB), slice(o + 2 * NB, BS)
        xf = split(xf)
        X1 = split(c_ref[near, o : o + NB])
        x_ref[:, near] = x_ref[:, near] - dot3(xf, X1, NT)
        if b < n - 2:
            X2 = dot3(split(a_ref[far, o : o + NB]), inv, NT)
            c_ref[far, o : o + NB] = X2
            X2 = split(X2)
            a_ref[far, near] = a_ref[far, near] - dot3(X2, X1, NT)
            a_ref[far, far] = a_ref[far, far] - dot3(X2, X2, NT)
            x_ref[:, far] = x_ref[:, far] - dot3(xf, X2, NT)

    T = [a_ref[8 * g : 8 * g + 8, 0:NB] for g in range(NB // 8)]
    left = None
    for b in range(n):
        o = b * NB
        out = eliminate(T)
        if left is not None:
            rest_of(*left)
        for g in range(NB // 8):
            i_ref[b, 8 * g : 8 * g + 8, :] = out[g]
        inv = split(i_ref[b])
        if b < n - 1:
            near = slice(o + NB, o + 2 * NB)
            X1 = dot3(split(a_ref[near, o : o + NB]), inv, NT)
            c_ref[near, o : o + NB] = X1
            X1 = split(X1)
            diagonal = a_ref[near, near] - dot3(X1, X1, NT)
            T = [diagonal[8 * g : 8 * g + 8, :] for g in range(NB // 8)]
        left = (b, o, inv)
    rest_of(*left)
    panel = px_ref[0:16, :]
    grow = rank * 16 + lax.broadcasted_iota(jnp.int32, (16, BS), 0)
    gcol = lax.broadcasted_iota(jnp.int32, (16, BS), 1)
    panel = jnp.where((is_corner == 1) & (gcol > grow), 0.0, panel)
    p_ref[...] = panel
    ws = [None] * n
    wv = [None] * n
    for b in reversed(range(n)):
        o = b * NB
        acc = px_ref[16:, o : o + NB]
        for i in range(b + 1, n):
            acc = acc - dot3(ws[i], split(c_ref[i * NB : (i + 1) * NB, o : o + NB]), NN)
        wv[b] = dot3(split(acc), split(i_ref[b]), NN)
        ws[b] = split(wv[b])
    for half in range(NC):

        @pl.when(core == half)
        def _():
            for q in range(2):
                w_ref[:, q * NB : (q + 1) * NB] = wv[2 * half + q]


def update_kernel(s_ref, w_ref, own_ref, r0_ref, r1_ref, r2_ref, rest_ref, mine_ref, other_ref):
    core = s_ref[CORE]
    for e, recv_ref in enumerate((r0_ref, r1_ref, r2_ref)):
        own = s_ref[OWN + e]
        cols = slice(e * BS, (e + 1) * BS)
        got = jnp.where(own == 1, own_ref[...], recv_ref[...])
        part = dot3(split(w_ref[16 * e : 16 * e + 16, :]), split(got), NT)
        part = rest_ref[:, cols] - part
        low, high = part[0:8, :], part[8:16, :]
        mine_ref[:, cols] = jnp.where(core == 0, low, high)
        other_ref[:, cols] = jnp.where(core == 0, high, low)


def finish_kernel(s_ref, panel_ref, mine_ref, other_ref, out_ref):
    core = s_ref[CORE]
    row = s_ref[RANK] * 16 + core * 8 + lax.broadcasted_iota(jnp.int32, (8, BS), 0)
    col = lax.broadcasted_iota(jnp.int32, (8, BS), 1)
    panel = jnp.where(core == 0, panel_ref[0:8, :], panel_ref[8:16, :])
    values = []
    for e in range(3):
        cols = slice(e * BS, (e + 1) * BS)
        value = (mine_ref[:, cols] + other_ref[:, cols]) * (1.0 / TOKENS)
        on_diagonal = s_ref[ROW_I + 1 + e] == s_ref[COL_J + e]
        values.append(value + jnp.where(on_diagonal & (row == col), DAMPING, 0.0))
    for slot in range(4):
        out = jnp.where(s_ref[PANEL_SLOT] == slot, panel, 0.0)
        for e in range(3):
            out = jnp.where((s_ref[SLOT + e] == slot) & (s_ref[LIVE + e] == 1), values[e], out)
        out_ref[:, slot * BS : (slot + 1) * BS] = out


def vmem(count):
    return [pl.BlockSpec(memory_space=pltpu.VMEM)] * count


SMEM = pl.BlockSpec(memory_space=pltpu.SMEM)


def params(limit=VMEM_LIMIT):
    return pltpu.CompilerParams(vmem_limit_bytes=limit)


def dp_index(z, y, c):
    return (z * NY + y) * NC + c


Z_GROUPS = [[dp_index(z, y, c) for z in range(NZ)] for y in range(NY) for c in range(NC)]
Y_GROUPS = [[dp_index(z, y, c) for y in range(NY)] for z in range(NZ) for c in range(NC)]
CORE_SWAP = [(dp_index(z, y, c), dp_index(z, y, 1 - c)) for z in range(NZ) for y in range(NY) for c in range(NC)]


def exchange(x, groups):
    return lax.all_to_all(x, "dp", 0, 0, axis_index_groups=groups)


def body(act):
    tok = act.shape[0]
    group = lax.axis_index("dp")
    place = lax.dynamic_index_in_dim(
        jnp.asarray(device_table()), group * NBLK + lax.axis_index("blk"), 0, keepdims=False
    )

    piece = jax.ShapeDtypeStruct((NZ, 72, HALF), F32)
    mine, other = pl.pallas_call(
        first_column_kernel,
        out_shape=[piece, piece],
        grid_spec=pltpu.PrefetchScalarGridSpec(
            num_scalar_prefetch=1,
            grid=(1,),
            in_specs=[
                pl.BlockSpec((tok, BS), lambda g, s: (0, 0)),
                pl.BlockSpec((tok, BS), lambda g, s: (0, s[HELD_AT])),
            ],
            out_specs=[pl.BlockSpec((NZ, 72, HALF), lambda g, s: (0, 0, 0))] * 2,
            scratch_shapes=[pltpu.VMEM((BS, BS), F32)],
        ),
        compiler_params=params(GRAM_LIMIT),
        name="first_column",
    )(place, act, act)
    first = mine + lax.ppermute(other, "dp", CORE_SWAP)
    over_z = exchange(first, Z_GROUPS)

    both = pl.pallas_call(
        trailing_kernel,
        out_shape=jax.ShapeDtypeStruct((BS, 3 * BS), F32),
        grid_spec=pltpu.PrefetchScalarGridSpec(
            num_scalar_prefetch=1,
            grid=(3,),
            in_specs=[
                pl.BlockSpec((tok, BS), lambda e, s: (0, s[ROW_I + 1 + e])),
                pl.BlockSpec((tok, BS), lambda e, s: (0, s[COL_J + e])),
                HBM,
            ],
            out_specs=pl.BlockSpec((BS, BS), lambda e, s: (0, e)),
        ),
        compiler_params=params(GRAM_LIMIT),
        cost_estimate=pl.CostEstimate(flops=4_000_000_000, bytes_accessed=7_000_000, transcendentals=0),
        name="trailing_gram",
    )(place, act, act, first)
    both = after(both, over_z)
    rest_z = lax.psum_scatter(both, "dp", scatter_dimension=0, tiled=True, axis_index_groups=Z_GROUPS)
    rest = lax.psum_scatter(rest_z, "dp", scatter_dimension=0, tiled=True, axis_index_groups=Y_GROUPS)

    spread = pl.pallas_call(
        sum_z_kernel,
        out_shape=jax.ShapeDtypeStruct((NY, 72, HALF), F32),
        in_specs=vmem(1),
        out_specs=vmem(1)[0],
        compiler_params=params(),
        name="sum_over_z",
    )(over_z)
    over_y = exchange(spread, Y_GROUPS)
    corner_rows, held_rows, own_rows = pl.pallas_call(
        sum_y_kernel,
        out_shape=[
            jax.ShapeDtypeStruct((NZ, 8, HALF), F32),
            jax.ShapeDtypeStruct((NZ, 64, HALF), F32),
            jax.ShapeDtypeStruct((16, HALF), F32),
        ],
        in_specs=[SMEM] + vmem(1),
        out_specs=vmem(3),
        compiler_params=params(),
        name="sum_over_y",
    )(place, over_y)

    corner_rows = exchange(corner_rows, Z_GROUPS)
    column = exchange(held_rows, Z_GROUPS).reshape(BS, HALF)
    share = jnp.concatenate([corner_rows.reshape(64, HALF), own_rows], axis=0)
    share = lax.all_to_all(jnp.broadcast_to(share, (NBLK, 80, HALF)), "blk", 0, 0)
    share_other = lax.ppermute(share, "dp", CORE_SWAP)
    sent = after(column, rest_z)
    brought = [lax.ppermute(sent, "blk", list(pairs)) for pairs in ROUNDS]

    panel, w = pl.pallas_call(
        corner_kernel,
        out_shape=[jax.ShapeDtypeStruct((16, BS), F32), jax.ShapeDtypeStruct((48, HALF), F32)],
        in_specs=[SMEM] + vmem(2),
        out_specs=vmem(2),
        scratch_shapes=[
            pltpu.VMEM((BS, BS), F32),
            pltpu.VMEM((BS, BS), F32),
            pltpu.VMEM((BS // NB, NB, NB), F32),
            pltpu.VMEM((64, BS), F32),
            pltpu.VMEM((64, BS), F32),
        ],
        compiler_params=params(),
        cost_estimate=pl.CostEstimate(flops=CORNER_FLOPS, bytes_accessed=2_000_000, transcendentals=0),
        name="corner",
    )(place, share, share_other)

    part = jax.ShapeDtypeStruct((8, 3 * BS), F32)
    mine, other = pl.pallas_call(
        update_kernel,
        out_shape=[part, part],
        in_specs=[SMEM] + vmem(6),
        out_specs=vmem(2),
        compiler_params=params(),
        name="update",
    )(place, w, sent, *brought, rest)
    return pl.pallas_call(
        finish_kernel,
        out_shape=jax.ShapeDtypeStruct((8, 4 * BS), F32),
        in_specs=[SMEM] + vmem(3),
        out_specs=vmem(1)[0],
        compiler_params=params(),
        name="finish",
    )(place, panel, mine, lax.ppermute(other, "dp", CORE_SWAP))


def solution(mesh):
    return jax.shard_map(body, mesh=mesh, in_specs=(P("dp", None),), out_specs=P("dp", "blk"), check_vma=False)
```

```python
import jax
import jax.numpy as jnp
import numpy as np
from jax import lax
from jax.experimental import pallas as pl
from jax.experimental.pallas import tpu as pltpu
from jax.sharding import PartitionSpec as P

BS = 512
HALF = 256
NB = 128
NZ, NY, NC, NBLK = 8, 4, 2, 8
TOKENS = 40960
DAMPING = 0.1
F32 = jnp.float32
VMEM_LIMIT = 40 * 1024 * 1024
GRAM_LIMIT = 60 * 1024 * 1024
CORNER_FLOPS = 200000000

HELD = (2, 1, 2, 3, 4, 5, 6, 1)
TRAIL = (
    ((6, 4), (2, 1), (5, 2)),
    ((5, 5), (6, 2), (3, 1)),
    ((3, 3), (6, 5), (4, 1)),
    ((6, 6), (5, 1), (4, 3)),
    ((6, 1), (5, 3), None),
    ((2, 2), None, (6, 3)),
    (None, (4, 4), (3, 2)),
    ((4, 2), (1, 1), (5, 4)),
)
ROUNDS = (
    ((3, 2), (4, 0), (5, 1), (6, 3), (7, 4), (2, 5), (0, 7)),
    ((3, 4), (4, 6), (5, 2), (1, 0), (7, 3), (0, 1)),
    ((3, 5), (4, 7), (1, 2), (2, 6)),
)


def owner_tables():
    count = BS * 7 // BS
    order = [(i, j) for j in range(count) for i in range(j, count)]
    slot_of = {pair: (t % NBLK, t // NBLK) for t, pair in enumerate(order)}
    rows = []
    for owner in range(NBLK):
        row = [HELD[owner], owner if 0 < owner < 7 else 1]
        for r in range(3):
            pair = TRAIL[owner][r]
            if pair is None:
                row += [1, 1, 0, 0, 0]
                continue
            at, slot = slot_of[pair]
            assert at == owner
            sent = [s for s, d in ROUNDS[r] if d == owner]
            own = 0 if sent else 1
            assert HELD[sent[0] if sent else owner] == pair[1]
            row += [pair[0], pair[1], 1, own, slot]
        rows.append(row)
    return np.asarray(rows, np.int32)


CORE, RANK, OWNER, HELD_AT, CORNER, ROW_I, COL_J, LIVE, OWN, SLOT, PANEL_SLOT = 0, 1, 2, 3, 4, 5, 9, 12, 15, 18, 21
WIDTH = 24


def device_table():
    per_owner = owner_tables()
    table = np.zeros((NZ * NY * NC * NBLK, WIDTH), np.int32)
    for group in range(NZ * NY * NC):
        for owner in range(NBLK):
            row = table[group * NBLK + owner]
            mine = per_owner[owner]
            row[CORE], row[RANK], row[OWNER] = group % NC, group // NC, owner
            row[HELD_AT], row[CORNER] = mine[0], owner == 0
            row[ROW_I] = mine[1]
            for e in range(3):
                i, j, live, own, slot = mine[2 + 5 * e : 7 + 5 * e]
                row[ROW_I + 1 + e], row[COL_J + e], row[LIVE + e], row[OWN + e], row[SLOT + e] = i, j, live, own, slot
            row[PANEL_SLOT] = 0 if owner < 7 else -1
    return table


def split(x):
    hi = x.astype(jnp.bfloat16)
    return hi, (x - hi.astype(F32)).astype(jnp.bfloat16)


def dot3(a, b, dims):
    def one(u, v):
        return lax.dot_general(u, v, (dims, ((), ())), preferred_element_type=F32)

    return one(a[0], b[0]) + (one(a[0], b[1]) + one(a[1], b[0]))


NT = ((1,), (1,))
NN = ((1,), (0,))
TN = ((0,), (0,))


def gram(a, b):
    return lax.dot_general(a, b, (TN, ((), ())), preferred_element_type=F32)


def first_column_kernel(s_ref, a0_ref, ai_ref, mine_ref, other_ref, d_ref):
    core = s_ref[CORE]
    owner = s_ref[OWNER]
    a0 = a0_ref[...]
    d_ref[...] = gram(a0, a0)
    for half in range(NC):
        block = gram(ai_ref[...], a0[:, half * HALF : (half + 1) * HALF])

        def store(out_ref):
            for z in range(NZ):
                row = pl.multiple_of(owner * 64 + z * 8, 8)
                out_ref[z, 0:8, :] = d_ref[pl.ds(row, 8), half * HALF : (half + 1) * HALF]
                out_ref[z, 8:72, :] = block[z * 64 : (z + 1) * 64, :]

        @pl.when(core == half)
        def _():
            store(mine_ref)

        @pl.when(core != half)
        def _():
            store(other_ref)


def sum_z_kernel(x_ref, out_ref, ready_ref):
    ready_ref[...] = jnp.zeros(ready_ref.shape, F32)
    total = x_ref[0]
    for z in range(1, NZ):
        total = total + x_ref[z]
    for y in range(NY):
        out_ref[y] = total


def sum_y_kernel(s_ref, x_ref, corner_ref, held_ref, rows_ref):
    total = x_ref[0]
    for y in range(1, NY):
        total = total + x_ref[y]
    for z in range(NZ):
        corner_ref[z] = total[0:8, :]
        held_ref[z] = total[8:72, :]
    for y in range(NY):

        @pl.when(lax.rem(s_ref[RANK], NY) == y)
        def _():
            rows_ref[...] = total[8 + 16 * y : 24 + 16 * y, :]


def pass_kernel(x_ref, after_ref, out_ref):
    del x_ref, after_ref, out_ref


HBM = pl.BlockSpec(memory_space=pltpu.HBM)


def after(x, dep, where=HBM):
    return pl.pallas_call(
        pass_kernel,
        out_shape=jax.ShapeDtypeStruct(x.shape, x.dtype),
        in_specs=[HBM, where],
        out_specs=HBM,
        input_output_aliases={0: 0},
        name="after",
    )(x, dep)


def trailing_kernel(s_ref, ai_ref, aj_ref, after_ref, out_ref):
    del s_ref, after_ref
    out_ref[...] = gram(ai_ref[...], aj_ref[...])


def recip(x):
    r = pl.reciprocal(x, approx=True)
    return r * (2.0 - x * r)


def lanes(x, c):
    return jnp.broadcast_to(x[:, c : c + 1], (8, NB))


def sublanes(x, k):
    return jnp.broadcast_to(x[k : k + 1, :], (8, NB))


def eliminate(T):
    n = len(T)
    T = list(T)
    lane = lax.broadcasted_iota(jnp.int32, (8, NB), 1)
    sub = lax.broadcasted_iota(jnp.int32, (8, NB), 0)
    out = [None] * n
    own = [lanes(T[0], k) for k in range(8)]
    for g in range(n):
        c0 = 8 * g
        last = g == n - 1
        V = list(own) + ([] if last else [lanes(T[g], c0 + 8 + k) for k in range(8)])
        if not last:
            A = [lanes(T[g + 1], c0 + k) for k in range(8)]
            U = [lanes(T[g + 1], c0 + 8 + k) for k in range(8)]
        ingroup = (lane >= c0) & (lane < c0 + 8)
        R = jnp.where(ingroup, jnp.where(lane == sub + c0, 1.0, 0.0), T[g])
        R1 = None if last else jnp.where(ingroup, 0.0, T[g + 1])
        rcp, d, rows = [], [], []
        pivot = jnp.ones((8, NB), F32)
        for k in range(8):
            dk = [sublanes(V[j], k) for j in range(k, len(V))]
            r = recip(dk[0])
            pivot = jnp.where(sub == k, dk[0], pivot)
            Rk = sublanes(R, k)
            rcp.append(r)
            d.append(dk)
            rows.append(Rk)
            if k < 7:
                m = jnp.where(sub > k, V[k], 0.0) * r
                for j in range(k + 1, len(V)):
                    V[j] = V[j] - m * dk[j - k]
                R = R - m * Rk
            if not last:
                m = A[k] * r
                for j in range(k + 1, 8):
                    A[j] = A[j] - m * dk[j - k]
                for j in range(8):
                    U[j] = U[j] - m * dk[8 + j - k]
                R1 = R1 - m * Rk
        out[g] = jnp.where(lane < c0 + 8, R * lax.rsqrt(pivot), 0.0)
        if not last:
            T[g + 1] = R1
            own = U
        for s in range(g + 2, n):
            W = [lanes(T[s], c0 + k) for k in range(8)]
            R = jnp.where(ingroup, 0.0, T[s])
            for k in range(8):
                m = W[k] * rcp[k]
                for j in range(k + 1, 8):
                    W[j] = W[j] - m * d[k][j - k]
                R = R - m * rows[k]
            T[s] = R
    return out


def corner_kernel(s_ref, mine_ref, other_ref, p_ref, w_ref, a_ref, c_ref, i_ref, x_ref, px_ref):
    core = s_ref[CORE]
    rank = s_ref[RANK]
    is_corner = s_ref[CORNER]
    n = BS // NB
    scale = 1.0 / TOKENS
    for half in range(NC):
        cols = slice(half * HALF, (half + 1) * HALF)

        def load(src_ref):
            for o in range(NBLK):
                a_ref[64 * o : 64 * o + 64, cols] = src_ref[o, 0:64, :] * scale
            for q in range(4):
                x_ref[16 * q : 16 * q + 16, cols] = src_ref[s_ref[ROW_I + q], 64:80, :] * scale

        @pl.when(core == half)
        def _():
            load(mine_ref)

        @pl.when(core != half)
        def _():
            load(other_ref)

    row = lax.broadcasted_iota(jnp.int32, (NB, NB), 0)
    col = lax.broadcasted_iota(jnp.int32, (NB, NB), 1)
    for b in range(n):
        at = slice(b * NB, (b + 1) * NB)
        a_ref[at, at] = a_ref[at, at] + jnp.where(row == col, DAMPING, 0.0)

    @pl.when(is_corner == 1)
    def _():
        x_ref[0:16, :] = a_ref[pl.ds(pl.multiple_of(rank * 16, 16), 16), :]

    def rest_of(b, o, inv):
        xf = dot3(split(x_ref[:, o : o + NB]), inv, NT)
        px_ref[:, o : o + NB] = xf
        if b == n - 1:
            return
        near, far = slice(o + NB, o + 2 * NB), slice(o + 2 * NB, BS)
        xf = split(xf)
        X1 = split(c_ref[near, o : o + NB])
        x_ref[:, near] = x_ref[:, near] - dot3(xf, X1, NT)
        if b < n - 2:
            X2 = dot3(split(a_ref[far, o : o + NB]), inv, NT)
            c_ref[far, o : o + NB] = X2
            X2 = split(X2)
            a_ref[far, near] = a_ref[far, near] - dot3(X2, X1, NT)
            a_ref[far, far] = a_ref[far, far] - dot3(X2, X2, NT)
            x_ref[:, far] = x_ref[:, far] - dot3(xf, X2, NT)

    T = [a_ref[8 * g : 8 * g + 8, 0:NB] for g in range(NB // 8)]
    left = None
    for b in range(n):
        o = b * NB
        out = eliminate(T)
        if left is not None:
            rest_of(*left)
        for g in range(NB // 8):
            i_ref[b, 8 * g : 8 * g + 8, :] = out[g]
        inv = split(i_ref[b])
        if b < n - 1:
            near = slice(o + NB, o + 2 * NB)
            X1 = dot3(split(a_ref[near, o : o + NB]), inv, NT)
            c_ref[near, o : o + NB] = X1
            X1 = split(X1)
            diagonal = a_ref[near, near] - dot3(X1, X1, NT)
            T = [diagonal[8 * g : 8 * g + 8, :] for g in range(NB // 8)]
        left = (b, o, inv)
    rest_of(*left)
    panel = px_ref[0:16, :]
    grow = rank * 16 + lax.broadcasted_iota(jnp.int32, (16, BS), 0)
    gcol = lax.broadcasted_iota(jnp.int32, (16, BS), 1)
    panel = jnp.where((is_corner == 1) & (gcol > grow), 0.0, panel)
    p_ref[...] = panel
    ws = [None] * n
    wv = [None] * n
    for b in reversed(range(n)):
        o = b * NB
        acc = px_ref[16:, o : o + NB]
        for i in range(b + 1, n):
            acc = acc - dot3(ws[i], split(c_ref[i * NB : (i + 1) * NB, o : o + NB]), NN)
        wv[b] = dot3(split(acc), split(i_ref[b]), NN)
        ws[b] = split(wv[b])
    for half in range(NC):

        @pl.when(core == half)
        def _():
            for q in range(2):
                w_ref[:, q * NB : (q + 1) * NB] = wv[2 * half + q]


def update_kernel(s_ref, w_ref, own_ref, r0_ref, r1_ref, r2_ref, rest_ref, mine_ref, other_ref):
    core = s_ref[CORE]
    for e, recv_ref in enumerate((r0_ref, r1_ref, r2_ref)):
        own = s_ref[OWN + e]
        cols = slice(e * BS, (e + 1) * BS)
        got = jnp.where(own == 1, own_ref[...], recv_ref[...])
        part = dot3(split(w_ref[16 * e : 16 * e + 16, :]), split(got), NT)
        part = rest_ref[:, cols] - part
        low, high = part[0:8, :], part[8:16, :]
        mine_ref[:, cols] = jnp.where(core == 0, low, high)
        other_ref[:, cols] = jnp.where(core == 0, high, low)


def finish_kernel(s_ref, panel_ref, mine_ref, other_ref, out_ref):
    core = s_ref[CORE]
    row = s_ref[RANK] * 16 + core * 8 + lax.broadcasted_iota(jnp.int32, (8, BS), 0)
    col = lax.broadcasted_iota(jnp.int32, (8, BS), 1)
    panel = jnp.where(core == 0, panel_ref[0:8, :], panel_ref[8:16, :])
    values = []
    for e in range(3):
        cols = slice(e * BS, (e + 1) * BS)
        value = (mine_ref[:, cols] + other_ref[:, cols]) * (1.0 / TOKENS)
        on_diagonal = s_ref[ROW_I + 1 + e] == s_ref[COL_J + e]
        values.append(value + jnp.where(on_diagonal & (row == col), DAMPING, 0.0))
    for slot in range(4):
        out = jnp.where(s_ref[PANEL_SLOT] == slot, panel, 0.0)
        for e in range(3):
            out = jnp.where((s_ref[SLOT + e] == slot) & (s_ref[LIVE + e] == 1), values[e], out)
        out_ref[:, slot * BS : (slot + 1) * BS] = out


def vmem(count):
    return [pl.BlockSpec(memory_space=pltpu.VMEM)] * count


SMEM = pl.BlockSpec(memory_space=pltpu.SMEM)


def params(limit=VMEM_LIMIT):
    return pltpu.CompilerParams(vmem_limit_bytes=limit)


def dp_index(z, y, c):
    return (z * NY + y) * NC + c


Z_GROUPS = [[dp_index(z, y, c) for z in range(NZ)] for y in range(NY) for c in range(NC)]
Y_GROUPS = [[dp_index(z, y, c) for y in range(NY)] for z in range(NZ) for c in range(NC)]
CORE_SWAP = [(dp_index(z, y, c), dp_index(z, y, 1 - c)) for z in range(NZ) for y in range(NY) for c in range(NC)]


def exchange(x, groups):
    return lax.all_to_all(x, "dp", 0, 0, axis_index_groups=groups)


def body(act):
    tok = act.shape[0]
    group = lax.axis_index("dp")
    place = lax.dynamic_index_in_dim(
        jnp.asarray(device_table()), group * NBLK + lax.axis_index("blk"), 0, keepdims=False
    )

    piece = jax.ShapeDtypeStruct((NZ, 72, HALF), F32)
    mine, other = pl.pallas_call(
        first_column_kernel,
        out_shape=[piece, piece],
        grid_spec=pltpu.PrefetchScalarGridSpec(
            num_scalar_prefetch=1,
            grid=(1,),
            in_specs=[
                pl.BlockSpec((tok, BS), lambda g, s: (0, 0)),
                pl.BlockSpec((tok, BS), lambda g, s: (0, s[HELD_AT])),
            ],
            out_specs=[pl.BlockSpec((NZ, 72, HALF), lambda g, s: (0, 0, 0))] * 2,
            scratch_shapes=[pltpu.VMEM((BS, BS), F32)],
        ),
        compiler_params=params(GRAM_LIMIT),
        name="first_column",
    )(place, act, act)
    first = mine + lax.ppermute(other, "dp", CORE_SWAP)
    over_z = exchange(first, Z_GROUPS)

    both = pl.pallas_call(
        trailing_kernel,
        out_shape=jax.ShapeDtypeStruct((BS, 3 * BS), F32),
        grid_spec=pltpu.PrefetchScalarGridSpec(
            num_scalar_prefetch=1,
            grid=(3,),
            in_specs=[
                pl.BlockSpec((tok, BS), lambda e, s: (0, s[ROW_I + 1 + e])),
                pl.BlockSpec((tok, BS), lambda e, s: (0, s[COL_J + e])),
                HBM,
            ],
            out_specs=pl.BlockSpec((BS, BS), lambda e, s: (0, e)),
        ),
        compiler_params=params(GRAM_LIMIT),
        cost_estimate=pl.CostEstimate(flops=4_000_000_000, bytes_accessed=7_000_000, transcendentals=0),
        name="trailing_gram",
    )(place, act, act, first)
    spread, ready = pl.pallas_call(
        sum_z_kernel,
        out_shape=[jax.ShapeDtypeStruct((NY, 72, HALF), F32), jax.ShapeDtypeStruct((8, NB), F32)],
        in_specs=vmem(1),
        out_specs=vmem(2),
        compiler_params=params(),
        name="sum_over_z",
    )(over_z)
    both = after(both, ready, vmem(1)[0])
    rest_z = lax.psum_scatter(both, "dp", scatter_dimension=0, tiled=True, axis_index_groups=Z_GROUPS)
    rest = lax.psum_scatter(rest_z, "dp", scatter_dimension=0, tiled=True, axis_index_groups=Y_GROUPS)
    over_y = exchange(spread, Y_GROUPS)
    corner_rows, held_rows, own_rows = pl.pallas_call(
        sum_y_kernel,
        out_shape=[
            jax.ShapeDtypeStruct((NZ, 8, HALF), F32),
            jax.ShapeDtypeStruct((NZ, 64, HALF), F32),
            jax.ShapeDtypeStruct((16, HALF), F32),
        ],
        in_specs=[SMEM] + vmem(1),
        out_specs=vmem(3),
        compiler_params=params(),
        name="sum_over_y",
    )(place, over_y)

    corner_rows = exchange(corner_rows, Z_GROUPS)
    column = exchange(held_rows, Z_GROUPS).reshape(BS, HALF)
    share = jnp.concatenate([corner_rows.reshape(64, HALF), own_rows], axis=0)
    share = lax.all_to_all(jnp.broadcast_to(share, (NBLK, 80, HALF)), "blk", 0, 0)
    share = after(share, rest_z)
    share_other = lax.ppermute(share, "dp", CORE_SWAP)
    brought = [lax.ppermute(column, "blk", list(pairs)) for pairs in ROUNDS]

    panel, w = pl.pallas_call(
        corner_kernel,
        out_shape=[jax.ShapeDtypeStruct((16, BS), F32), jax.ShapeDtypeStruct((48, HALF), F32)],
        in_specs=[SMEM] + vmem(2),
        out_specs=vmem(2),
        scratch_shapes=[
            pltpu.VMEM((BS, BS), F32),
            pltpu.VMEM((BS, BS), F32),
            pltpu.VMEM((BS // NB, NB, NB), F32),
            pltpu.VMEM((64, BS), F32),
            pltpu.VMEM((64, BS), F32),
        ],
        compiler_params=params(),
        cost_estimate=pl.CostEstimate(flops=CORNER_FLOPS, bytes_accessed=2_000_000, transcendentals=0),
        name="corner",
    )(place, share, share_other)

    part = jax.ShapeDtypeStruct((8, 3 * BS), F32)
    mine, other = pl.pallas_call(
        update_kernel,
        out_shape=[part, part],
        in_specs=[SMEM] + vmem(6),
        out_specs=vmem(2),
        compiler_params=params(),
        name="update",
    )(place, w, column, *brought, rest)
    return pl.pallas_call(
        finish_kernel,
        out_shape=jax.ShapeDtypeStruct((8, 4 * BS), F32),
        in_specs=[SMEM] + vmem(3),
        out_specs=vmem(1)[0],
        compiler_params=params(),
        name="finish",
    )(place, panel, mine, lax.ppermute(other, "dp", CORE_SWAP))


def solution(mesh):
    return jax.shard_map(body, mesh=mesh, in_specs=(P("dp", None),), out_specs=P("dp", "blk"), check_vma=False)
```

```python
import jax
import jax.numpy as jnp
import numpy as np
from jax import lax
from jax.experimental import pallas as pl
from jax.experimental.pallas import tpu as pltpu
from jax.sharding import PartitionSpec as P

BS = 512
HALF = 256
NB = 128
NZ, NY, NC, NBLK = 8, 4, 2, 8
TOKENS = 40960
DAMPING = 0.1
F32 = jnp.float32
VMEM_LIMIT = 40 * 1024 * 1024
GRAM_LIMIT = 60 * 1024 * 1024
CORNER_FLOPS = 200000000

HELD = (2, 1, 2, 3, 4, 5, 6, 1)
TRAIL = (
    ((6, 4), (2, 1), (5, 2)),
    ((5, 5), (6, 2), (3, 1)),
    ((3, 3), (6, 5), (4, 1)),
    ((6, 6), (5, 1), (4, 3)),
    ((6, 1), (5, 3), None),
    ((2, 2), None, (6, 3)),
    (None, (4, 4), (3, 2)),
    ((4, 2), (1, 1), (5, 4)),
)
ROUNDS = (
    ((3, 2), (4, 0), (5, 1), (6, 3), (7, 4), (2, 5), (0, 7)),
    ((3, 4), (4, 6), (5, 2), (1, 0), (7, 3), (0, 1)),
    ((3, 5), (4, 7), (1, 2), (2, 6)),
)


def owner_tables():
    count = BS * 7 // BS
    order = [(i, j) for j in range(count) for i in range(j, count)]
    slot_of = {pair: (t % NBLK, t // NBLK) for t, pair in enumerate(order)}
    rows = []
    for owner in range(NBLK):
        row = [HELD[owner], owner if 0 < owner < 7 else 1]
        for r in range(3):
            pair = TRAIL[owner][r]
            if pair is None:
                row += [1, 1, 0, 0, 0]
                continue
            at, slot = slot_of[pair]
            assert at == owner
            sent = [s for s, d in ROUNDS[r] if d == owner]
            own = 0 if sent else 1
            assert HELD[sent[0] if sent else owner] == pair[1]
            row += [pair[0], pair[1], 1, own, slot]
        rows.append(row)
    return np.asarray(rows, np.int32)


CORE, RANK, OWNER, HELD_AT, CORNER, ROW_I, COL_J, LIVE, OWN, SLOT, PANEL_SLOT = 0, 1, 2, 3, 4, 5, 9, 12, 15, 18, 21
WIDTH = 24


def device_table():
    per_owner = owner_tables()
    table = np.zeros((NZ * NY * NC * NBLK, WIDTH), np.int32)
    for group in range(NZ * NY * NC):
        for owner in range(NBLK):
            row = table[group * NBLK + owner]
            mine = per_owner[owner]
            row[CORE], row[RANK], row[OWNER] = group % NC, group // NC, owner
            row[HELD_AT], row[CORNER] = mine[0], owner == 0
            row[ROW_I] = mine[1]
            for e in range(3):
                i, j, live, own, slot = mine[2 + 5 * e : 7 + 5 * e]
                row[ROW_I + 1 + e], row[COL_J + e], row[LIVE + e], row[OWN + e], row[SLOT + e] = i, j, live, own, slot
            row[PANEL_SLOT] = 0 if owner < 7 else -1
    return table


def split(x):
    hi = x.astype(jnp.bfloat16)
    return hi, (x - hi.astype(F32)).astype(jnp.bfloat16)


def dot3(a, b, dims):
    def one(u, v):
        return lax.dot_general(u, v, (dims, ((), ())), preferred_element_type=F32)

    return one(a[0], b[0]) + (one(a[0], b[1]) + one(a[1], b[0]))


NT = ((1,), (1,))
NN = ((1,), (0,))
TN = ((0,), (0,))


def gram(a, b):
    return lax.dot_general(a, b, (TN, ((), ())), preferred_element_type=F32)


def first_column_kernel(s_ref, a0_ref, ai_ref, mine_ref, other_ref, d_ref):
    core = s_ref[CORE]
    owner = s_ref[OWNER]
    a0 = a0_ref[...]
    d_ref[...] = gram(a0, a0)
    for half in range(NC):
        block = gram(ai_ref[...], a0[:, half * HALF : (half + 1) * HALF])

        def store(out_ref):
            for z in range(NZ):
                row = pl.multiple_of(owner * 64 + z * 8, 8)
                out_ref[z, 0:8, :] = d_ref[pl.ds(row, 8), half * HALF : (half + 1) * HALF]
                out_ref[z, 8:72, :] = block[z * 64 : (z + 1) * 64, :]

        @pl.when(core == half)
        def _():
            store(mine_ref)

        @pl.when(core != half)
        def _():
            store(other_ref)


def sum_z_kernel(x_ref, out_ref, ready_ref):
    ready_ref[...] = jnp.zeros(ready_ref.shape, F32)
    total = x_ref[0]
    for z in range(1, NZ):
        total = total + x_ref[z]
    for y in range(NY):
        out_ref[y] = total


def sum_y_kernel(s_ref, x_ref, corner_ref, held_ref, rows_ref):
    total = x_ref[0]
    for y in range(1, NY):
        total = total + x_ref[y]
    for z in range(NZ):
        corner_ref[z] = total[0:8, :]
        held_ref[z] = total[8:72, :]
    for y in range(NY):

        @pl.when(lax.rem(s_ref[RANK], NY) == y)
        def _():
            rows_ref[...] = total[8 + 16 * y : 24 + 16 * y, :]


def pass_kernel(x_ref, after_ref, out_ref):
    del x_ref, after_ref, out_ref


HBM = pl.BlockSpec(memory_space=pltpu.HBM)


def after(x, dep, where=HBM):
    return pl.pallas_call(
        pass_kernel,
        out_shape=jax.ShapeDtypeStruct(x.shape, x.dtype),
        in_specs=[HBM, where],
        out_specs=HBM,
        input_output_aliases={0: 0},
        cost_estimate=pl.CostEstimate(flops=0, bytes_accessed=0, transcendentals=0),
        name="after",
    )(x, dep)


def trailing_kernel(s_ref, ai_ref, aj_ref, after_ref, out_ref):
    del s_ref, after_ref
    out_ref[...] = gram(ai_ref[...], aj_ref[...])


def recip(x):
    r = pl.reciprocal(x, approx=True)
    return r * (2.0 - x * r)


def lanes(x, c):
    return jnp.broadcast_to(x[:, c : c + 1], (8, NB))


def sublanes(x, k):
    return jnp.broadcast_to(x[k : k + 1, :], (8, NB))


def eliminate(T):
    n = len(T)
    T = list(T)
    lane = lax.broadcasted_iota(jnp.int32, (8, NB), 1)
    sub = lax.broadcasted_iota(jnp.int32, (8, NB), 0)
    out = [None] * n
    own = [lanes(T[0], k) for k in range(8)]
    for g in range(n):
        c0 = 8 * g
        last = g == n - 1
        V = list(own) + ([] if last else [lanes(T[g], c0 + 8 + k) for k in range(8)])
        if not last:
            A = [lanes(T[g + 1], c0 + k) for k in range(8)]
            U = [lanes(T[g + 1], c0 + 8 + k) for k in range(8)]
        ingroup = (lane >= c0) & (lane < c0 + 8)
        R = jnp.where(ingroup, jnp.where(lane == sub + c0, 1.0, 0.0), T[g])
        R1 = None if last else jnp.where(ingroup, 0.0, T[g + 1])
        rcp, d, rows = [], [], []
        pivot = jnp.ones((8, NB), F32)
        for k in range(8):
            dk = [sublanes(V[j], k) for j in range(k, len(V))]
            r = recip(dk[0])
            pivot = jnp.where(sub == k, dk[0], pivot)
            Rk = sublanes(R, k)
            rcp.append(r)
            d.append(dk)
            rows.append(Rk)
            if k < 7:
                m = jnp.where(sub > k, V[k], 0.0) * r
                for j in range(k + 1, len(V)):
                    V[j] = V[j] - m * dk[j - k]
                R = R - m * Rk
            if not last:
                m = A[k] * r
                for j in range(k + 1, 8):
                    A[j] = A[j] - m * dk[j - k]
                for j in range(8):
                    U[j] = U[j] - m * dk[8 + j - k]
                R1 = R1 - m * Rk
        out[g] = jnp.where(lane < c0 + 8, R * lax.rsqrt(pivot), 0.0)
        if not last:
            T[g + 1] = R1
            own = U
        for s in range(g + 2, n):
            W = [lanes(T[s], c0 + k) for k in range(8)]
            R = jnp.where(ingroup, 0.0, T[s])
            for k in range(8):
                m = W[k] * rcp[k]
                for j in range(k + 1, 8):
                    W[j] = W[j] - m * d[k][j - k]
                R = R - m * rows[k]
            T[s] = R
    return out


def corner_kernel(s_ref, mine_ref, other_ref, p_ref, w_ref, a_ref, c_ref, i_ref, x_ref, px_ref):
    core = s_ref[CORE]
    rank = s_ref[RANK]
    is_corner = s_ref[CORNER]
    n = BS // NB
    scale = 1.0 / TOKENS
    for half in range(NC):
        cols = slice(half * HALF, (half + 1) * HALF)

        def load(src_ref):
            for o in range(NBLK):
                a_ref[64 * o : 64 * o + 64, cols] = src_ref[o, 0:64, :] * scale
            for q in range(4):
                x_ref[16 * q : 16 * q + 16, cols] = src_ref[s_ref[ROW_I + q], 64:80, :] * scale

        @pl.when(core == half)
        def _():
            load(mine_ref)

        @pl.when(core != half)
        def _():
            load(other_ref)

    row = lax.broadcasted_iota(jnp.int32, (NB, NB), 0)
    col = lax.broadcasted_iota(jnp.int32, (NB, NB), 1)
    for b in range(n):
        at = slice(b * NB, (b + 1) * NB)
        a_ref[at, at] = a_ref[at, at] + jnp.where(row == col, DAMPING, 0.0)

    @pl.when(is_corner == 1)
    def _():
        x_ref[0:16, :] = a_ref[pl.ds(pl.multiple_of(rank * 16, 16), 16), :]

    def rest_of(b, o, inv):
        xf = dot3(split(x_ref[:, o : o + NB]), inv, NT)
        px_ref[:, o : o + NB] = xf
        if b == n - 1:
            return
        near, far = slice(o + NB, o + 2 * NB), slice(o + 2 * NB, BS)
        xf = split(xf)
        X1 = split(c_ref[near, o : o + NB])
        x_ref[:, near] = x_ref[:, near] - dot3(xf, X1, NT)
        if b < n - 2:
            X2 = dot3(split(a_ref[far, o : o + NB]), inv, NT)
            c_ref[far, o : o + NB] = X2
            X2 = split(X2)
            a_ref[far, near] = a_ref[far, near] - dot3(X2, X1, NT)
            a_ref[far, far] = a_ref[far, far] - dot3(X2, X2, NT)
            x_ref[:, far] = x_ref[:, far] - dot3(xf, X2, NT)

    T = [a_ref[8 * g : 8 * g + 8, 0:NB] for g in range(NB // 8)]
    left = None
    for b in range(n):
        o = b * NB
        out = eliminate(T)
        if left is not None:
            rest_of(*left)
        for g in range(NB // 8):
            i_ref[b, 8 * g : 8 * g + 8, :] = out[g]
        inv = split(i_ref[b])
        if b < n - 1:
            near = slice(o + NB, o + 2 * NB)
            X1 = dot3(split(a_ref[near, o : o + NB]), inv, NT)
            c_ref[near, o : o + NB] = X1
            X1 = split(X1)
            diagonal = a_ref[near, near] - dot3(X1, X1, NT)
            T = [diagonal[8 * g : 8 * g + 8, :] for g in range(NB // 8)]
        left = (b, o, inv)
    rest_of(*left)
    panel = px_ref[0:16, :]
    grow = rank * 16 + lax.broadcasted_iota(jnp.int32, (16, BS), 0)
    gcol = lax.broadcasted_iota(jnp.int32, (16, BS), 1)
    panel = jnp.where((is_corner == 1) & (gcol > grow), 0.0, panel)
    p_ref[...] = panel
    ws = [None] * n
    wv = [None] * n
    for b in reversed(range(n)):
        o = b * NB
        acc = px_ref[16:, o : o + NB]
        for i in range(b + 1, n):
            acc = acc - dot3(ws[i], split(c_ref[i * NB : (i + 1) * NB, o : o + NB]), NN)
        wv[b] = dot3(split(acc), split(i_ref[b]), NN)
        ws[b] = split(wv[b])
    for half in range(NC):

        @pl.when(core == half)
        def _():
            for q in range(2):
                w_ref[:, q * NB : (q + 1) * NB] = wv[2 * half + q]


def update_kernel(s_ref, w_ref, own_ref, r0_ref, r1_ref, r2_ref, rest_ref, mine_ref, other_ref):
    core = s_ref[CORE]
    for e, recv_ref in enumerate((r0_ref, r1_ref, r2_ref)):
        own = s_ref[OWN + e]
        cols = slice(e * BS, (e + 1) * BS)
        got = jnp.where(own == 1, own_ref[...], recv_ref[...])
        part = dot3(split(w_ref[16 * e : 16 * e + 16, :]), split(got), NT)
        part = rest_ref[:, cols] - part
        low, high = part[0:8, :], part[8:16, :]
        mine_ref[:, cols] = jnp.where(core == 0, low, high)
        other_ref[:, cols] = jnp.where(core == 0, high, low)


def finish_kernel(s_ref, panel_ref, mine_ref, other_ref, out_ref):
    core = s_ref[CORE]
    row = s_ref[RANK] * 16 + core * 8 + lax.broadcasted_iota(jnp.int32, (8, BS), 0)
    col = lax.broadcasted_iota(jnp.int32, (8, BS), 1)
    panel = jnp.where(core == 0, panel_ref[0:8, :], panel_ref[8:16, :])
    values = []
    for e in range(3):
        cols = slice(e * BS, (e + 1) * BS)
        value = (mine_ref[:, cols] + other_ref[:, cols]) * (1.0 / TOKENS)
        on_diagonal = s_ref[ROW_I + 1 + e] == s_ref[COL_J + e]
        values.append(value + jnp.where(on_diagonal & (row == col), DAMPING, 0.0))
    for slot in range(4):
        out = jnp.where(s_ref[PANEL_SLOT] == slot, panel, 0.0)
        for e in range(3):
            out = jnp.where((s_ref[SLOT + e] == slot) & (s_ref[LIVE + e] == 1), values[e], out)
        out_ref[:, slot * BS : (slot + 1) * BS] = out


def vmem(count):
    return [pl.BlockSpec(memory_space=pltpu.VMEM)] * count


SMEM = pl.BlockSpec(memory_space=pltpu.SMEM)


def params(limit=VMEM_LIMIT):
    return pltpu.CompilerParams(vmem_limit_bytes=limit)


def dp_index(z, y, c):
    return (z * NY + y) * NC + c


Z_GROUPS = [[dp_index(z, y, c) for z in range(NZ)] for y in range(NY) for c in range(NC)]
Y_GROUPS = [[dp_index(z, y, c) for y in range(NY)] for z in range(NZ) for c in range(NC)]
CORE_SWAP = [(dp_index(z, y, c), dp_index(z, y, 1 - c)) for z in range(NZ) for y in range(NY) for c in range(NC)]


def exchange(x, groups):
    return lax.all_to_all(x, "dp", 0, 0, axis_index_groups=groups)


def body(act):
    tok = act.shape[0]
    group = lax.axis_index("dp")
    place = lax.dynamic_index_in_dim(
        jnp.asarray(device_table()), group * NBLK + lax.axis_index("blk"), 0, keepdims=False
    )

    piece = jax.ShapeDtypeStruct((NZ, 72, HALF), F32)
    mine, other = pl.pallas_call(
        first_column_kernel,
        out_shape=[piece, piece],
        grid_spec=pltpu.PrefetchScalarGridSpec(
            num_scalar_prefetch=1,
            grid=(1,),
            in_specs=[
                pl.BlockSpec((tok, BS), lambda g, s: (0, 0)),
                pl.BlockSpec((tok, BS), lambda g, s: (0, s[HELD_AT])),
            ],
            out_specs=[pl.BlockSpec((NZ, 72, HALF), lambda g, s: (0, 0, 0))] * 2,
            scratch_shapes=[pltpu.VMEM((BS, BS), F32)],
        ),
        compiler_params=params(GRAM_LIMIT),
        name="first_column",
    )(place, act, act)
    first = mine + lax.ppermute(other, "dp", CORE_SWAP)
    over_z = exchange(first, Z_GROUPS)

    both = pl.pallas_call(
        trailing_kernel,
        out_shape=jax.ShapeDtypeStruct((BS, 3 * BS), F32),
        grid_spec=pltpu.PrefetchScalarGridSpec(
            num_scalar_prefetch=1,
            grid=(3,),
            in_specs=[
                pl.BlockSpec((tok, BS), lambda e, s: (0, s[ROW_I + 1 + e])),
                pl.BlockSpec((tok, BS), lambda e, s: (0, s[COL_J + e])),
                HBM,
            ],
            out_specs=pl.BlockSpec((BS, BS), lambda e, s: (0, e)),
        ),
        compiler_params=params(GRAM_LIMIT),
        cost_estimate=pl.CostEstimate(flops=4_000_000_000, bytes_accessed=7_000_000, transcendentals=0),
        name="trailing_gram",
    )(place, act, act, first)
    spread, ready = pl.pallas_call(
        sum_z_kernel,
        out_shape=[jax.ShapeDtypeStruct((NY, 72, HALF), F32), jax.ShapeDtypeStruct((8, NB), F32)],
        in_specs=vmem(1),
        out_specs=vmem(2),
        compiler_params=params(),
        name="sum_over_z",
    )(over_z)
    both = after(both, ready, vmem(1)[0])
    rest_z = lax.psum_scatter(both, "dp", scatter_dimension=0, tiled=True, axis_index_groups=Z_GROUPS)
    rest = lax.psum_scatter(rest_z, "dp", scatter_dimension=0, tiled=True, axis_index_groups=Y_GROUPS)
    over_y = exchange(spread, Y_GROUPS)
    corner_rows, held_rows, own_rows = pl.pallas_call(
        sum_y_kernel,
        out_shape=[
            jax.ShapeDtypeStruct((NZ, 8, HALF), F32),
            jax.ShapeDtypeStruct((NZ, 64, HALF), F32),
            jax.ShapeDtypeStruct((16, HALF), F32),
        ],
        in_specs=[SMEM] + vmem(1),
        out_specs=vmem(3),
        compiler_params=params(),
        name="sum_over_y",
    )(place, over_y)

    corner_rows = exchange(corner_rows, Z_GROUPS)
    column = exchange(held_rows, Z_GROUPS).reshape(BS, HALF)
    share = jnp.concatenate([corner_rows.reshape(64, HALF), own_rows], axis=0)
    share = lax.all_to_all(jnp.broadcast_to(share, (NBLK, 80, HALF)), "blk", 0, 0)
    share_other = lax.ppermute(share, "dp", CORE_SWAP)
    brought = [lax.ppermute(column, "blk", list(pairs)) for pairs in ROUNDS]

    panel, w = pl.pallas_call(
        corner_kernel,
        out_shape=[jax.ShapeDtypeStruct((16, BS), F32), jax.ShapeDtypeStruct((48, HALF), F32)],
        in_specs=[SMEM] + vmem(2),
        out_specs=vmem(2),
        scratch_shapes=[
            pltpu.VMEM((BS, BS), F32),
            pltpu.VMEM((BS, BS), F32),
            pltpu.VMEM((BS // NB, NB, NB), F32),
            pltpu.VMEM((64, BS), F32),
            pltpu.VMEM((64, BS), F32),
        ],
        compiler_params=params(),
        cost_estimate=pl.CostEstimate(flops=CORNER_FLOPS, bytes_accessed=2_000_000, transcendentals=0),
        name="corner",
    )(place, share, share_other)

    part = jax.ShapeDtypeStruct((8, 3 * BS), F32)
    mine, other = pl.pallas_call(
        update_kernel,
        out_shape=[part, part],
        in_specs=[SMEM] + vmem(6),
        out_specs=vmem(2),
        compiler_params=params(),
        name="update",
    )(place, w, column, *brought, rest)
    return pl.pallas_call(
        finish_kernel,
        out_shape=jax.ShapeDtypeStruct((8, 4 * BS), F32),
        in_specs=[SMEM] + vmem(3),
        out_specs=vmem(1)[0],
        compiler_params=params(),
        name="finish",
    )(place, panel, mine, lax.ppermute(other, "dp", CORE_SWAP))


def solution(mesh):
    return jax.shard_map(body, mesh=mesh, in_specs=(P("dp", None),), out_specs=P("dp", "blk"), check_vma=False)
```

```python
import jax
import jax.numpy as jnp
import numpy as np
from jax import lax
from jax.experimental import pallas as pl
from jax.experimental.pallas import tpu as pltpu
from jax.sharding import PartitionSpec as P

BS = 512
HALF = 256
NB = 128
NZ, NY, NC, NBLK = 8, 4, 2, 8
TOKENS = 40960
DAMPING = 0.1
F32 = jnp.float32
VMEM_LIMIT = 40 * 1024 * 1024
GRAM_LIMIT = 60 * 1024 * 1024
CORNER_FLOPS = 200000000

HELD = (2, 1, 2, 3, 4, 5, 6, 1)
TRAIL = (
    ((6, 4), (2, 1), (5, 2)),
    ((5, 5), (6, 2), (3, 1)),
    ((3, 3), (6, 5), (4, 1)),
    ((6, 6), (5, 1), (4, 3)),
    ((6, 1), (5, 3), None),
    ((2, 2), None, (6, 3)),
    (None, (4, 4), (3, 2)),
    ((4, 2), (1, 1), (5, 4)),
)
ROUNDS = (
    ((3, 2), (4, 0), (5, 1), (6, 3), (7, 4), (2, 5), (0, 7)),
    ((3, 4), (4, 6), (5, 2), (1, 0), (7, 3), (0, 1)),
    ((3, 5), (4, 7), (1, 2), (2, 6)),
)


def owner_tables():
    count = BS * 7 // BS
    order = [(i, j) for j in range(count) for i in range(j, count)]
    slot_of = {pair: (t % NBLK, t // NBLK) for t, pair in enumerate(order)}
    rows = []
    for owner in range(NBLK):
        row = [HELD[owner], owner if 0 < owner < 7 else 1]
        for r in range(3):
            pair = TRAIL[owner][r]
            if pair is None:
                row += [1, 1, 0, 0, 0]
                continue
            at, slot = slot_of[pair]
            assert at == owner
            sent = [s for s, d in ROUNDS[r] if d == owner]
            own = 0 if sent else 1
            assert HELD[sent[0] if sent else owner] == pair[1]
            row += [pair[0], pair[1], 1, own, slot]
        rows.append(row)
    return np.asarray(rows, np.int32)


CORE, RANK, OWNER, HELD_AT, CORNER, ROW_I, COL_J, LIVE, OWN, SLOT, PANEL_SLOT = 0, 1, 2, 3, 4, 5, 9, 12, 15, 18, 21
WIDTH = 24


def device_table():
    per_owner = owner_tables()
    table = np.zeros((NZ * NY * NC * NBLK, WIDTH), np.int32)
    for group in range(NZ * NY * NC):
        for owner in range(NBLK):
            row = table[group * NBLK + owner]
            mine = per_owner[owner]
            row[CORE], row[RANK], row[OWNER] = group % NC, group // NC, owner
            row[HELD_AT], row[CORNER] = mine[0], owner == 0
            row[ROW_I] = mine[1]
            for e in range(3):
                i, j, live, own, slot = mine[2 + 5 * e : 7 + 5 * e]
                row[ROW_I + 1 + e], row[COL_J + e], row[LIVE + e], row[OWN + e], row[SLOT + e] = i, j, live, own, slot
            row[PANEL_SLOT] = 0 if owner < 7 else -1
    return table


def split(x):
    hi = x.astype(jnp.bfloat16)
    return hi, (x - hi.astype(F32)).astype(jnp.bfloat16)


def dot3(a, b, dims):
    def one(u, v):
        return lax.dot_general(u, v, (dims, ((), ())), preferred_element_type=F32)

    return one(a[0], b[0]) + (one(a[0], b[1]) + one(a[1], b[0]))


NT = ((1,), (1,))
NN = ((1,), (0,))
TN = ((0,), (0,))


def gram(a, b):
    return lax.dot_general(a, b, (TN, ((), ())), preferred_element_type=F32)


def first_column_kernel(s_ref, a0_ref, ai_ref, mine_ref, other_ref, d_ref):
    core = s_ref[CORE]
    owner = s_ref[OWNER]
    a0 = a0_ref[...]
    d_ref[...] = gram(a0, a0)
    for half in range(NC):
        block = gram(ai_ref[...], a0[:, half * HALF : (half + 1) * HALF])

        def store(out_ref):
            for z in range(NZ):
                row = pl.multiple_of(owner * 64 + z * 8, 8)
                out_ref[z, 0:8, :] = d_ref[pl.ds(row, 8), half * HALF : (half + 1) * HALF]
                out_ref[z, 8:72, :] = block[z * 64 : (z + 1) * 64, :]

        @pl.when(core == half)
        def _():
            store(mine_ref)

        @pl.when(core != half)
        def _():
            store(other_ref)


def sum_z_kernel(x_ref, out_ref, ready_ref):
    ready_ref[...] = jnp.zeros(ready_ref.shape, F32)
    total = x_ref[0]
    for z in range(1, NZ):
        total = total + x_ref[z]
    for y in range(NY):
        out_ref[y] = total


def sum_y_kernel(s_ref, x_ref, corner_ref, held_ref, rows_ref):
    total = x_ref[0]
    for y in range(1, NY):
        total = total + x_ref[y]
    for z in range(NZ):
        corner_ref[z] = total[0:8, :]
        held_ref[z] = total[8:72, :]
    for y in range(NY):

        @pl.when(lax.rem(s_ref[RANK], NY) == y)
        def _():
            rows_ref[...] = total[8 + 16 * y : 24 + 16 * y, :]


def pass_kernel(x_ref, after_ref, out_ref):
    del x_ref, after_ref, out_ref


HBM = pl.BlockSpec(memory_space=pltpu.HBM)


def after(x, dep, where=HBM):
    return pl.pallas_call(
        pass_kernel,
        out_shape=jax.ShapeDtypeStruct(x.shape, x.dtype),
        in_specs=[HBM, where],
        out_specs=HBM,
        input_output_aliases={0: 0},
        cost_estimate=pl.CostEstimate(flops=0, bytes_accessed=0, transcendentals=0),
        name="after",
    )(x, dep)


def trailing_kernel(s_ref, ai_ref, aj_ref, after_ref, out_ref):
    del s_ref, after_ref
    out_ref[...] = gram(ai_ref[...], aj_ref[...])


def recip(x):
    r = pl.reciprocal(x, approx=True)
    return r * (2.0 - x * r)


def lanes(x, c):
    return jnp.broadcast_to(x[:, c : c + 1], (8, NB))


def sublanes(x, k):
    return jnp.broadcast_to(x[k : k + 1, :], (8, NB))


def eliminate(T):
    n = len(T)
    T = list(T)
    lane = lax.broadcasted_iota(jnp.int32, (8, NB), 1)
    sub = lax.broadcasted_iota(jnp.int32, (8, NB), 0)
    out = [None] * n
    own = [lanes(T[0], k) for k in range(8)]
    for g in range(n):
        c0 = 8 * g
        last = g == n - 1
        V = list(own) + ([] if last else [lanes(T[g], c0 + 8 + k) for k in range(8)])
        if not last:
            A = [lanes(T[g + 1], c0 + k) for k in range(8)]
            U = [lanes(T[g + 1], c0 + 8 + k) for k in range(8)]
        ingroup = (lane >= c0) & (lane < c0 + 8)
        R = jnp.where(ingroup, jnp.where(lane == sub + c0, 1.0, 0.0), T[g])
        R1 = None if last else jnp.where(ingroup, 0.0, T[g + 1])
        rcp, d, rows = [], [], []
        pivot = jnp.ones((8, NB), F32)
        for k in range(8):
            dk = [sublanes(V[j], k) for j in range(k, len(V))]
            r = recip(dk[0])
            pivot = jnp.where(sub == k, dk[0], pivot)
            Rk = sublanes(R, k)
            rcp.append(r)
            d.append(dk)
            rows.append(Rk)
            if k < 7:
                m = jnp.where(sub > k, V[k], 0.0) * r
                for j in range(k + 1, len(V)):
                    V[j] = V[j] - m * dk[j - k]
                R = R - m * Rk
            if not last:
                m = A[k] * r
                for j in range(k + 1, 8):
                    A[j] = A[j] - m * dk[j - k]
                for j in range(8):
                    U[j] = U[j] - m * dk[8 + j - k]
                R1 = R1 - m * Rk
        out[g] = jnp.where(lane < c0 + 8, R * lax.rsqrt(pivot), 0.0)
        if not last:
            T[g + 1] = R1
            own = U
        for s in range(g + 2, n):
            W = [lanes(T[s], c0 + k) for k in range(8)]
            R = jnp.where(ingroup, 0.0, T[s])
            for k in range(8):
                m = W[k] * rcp[k]
                for j in range(k + 1, 8):
                    W[j] = W[j] - m * d[k][j - k]
                R = R - m * rows[k]
            T[s] = R
    return out


def corner_kernel(s_ref, mine_ref, other_ref, p_ref, w_ref, a_ref, c_ref, i_ref, x_ref, px_ref):
    core = s_ref[CORE]
    rank = s_ref[RANK]
    is_corner = s_ref[CORNER]
    n = BS // NB
    scale = 1.0 / TOKENS
    for half in range(NC):
        cols = slice(half * HALF, (half + 1) * HALF)

        def load(src_ref):
            for o in range(NBLK):
                a_ref[64 * o : 64 * o + 64, cols] = src_ref[o, 0:64, :] * scale
            for q in range(4):
                x_ref[16 * q : 16 * q + 16, cols] = src_ref[s_ref[ROW_I + q], 64:80, :] * scale

        @pl.when(core == half)
        def _():
            load(mine_ref)

        @pl.when(core != half)
        def _():
            load(other_ref)

    row = lax.broadcasted_iota(jnp.int32, (NB, NB), 0)
    col = lax.broadcasted_iota(jnp.int32, (NB, NB), 1)
    for b in range(n):
        at = slice(b * NB, (b + 1) * NB)
        a_ref[at, at] = a_ref[at, at] + jnp.where(row == col, DAMPING, 0.0)

    @pl.when(is_corner == 1)
    def _():
        x_ref[0:16, :] = a_ref[pl.ds(pl.multiple_of(rank * 16, 16), 16), :]

    def rest_of(b, o, inv):
        xf = dot3(split(x_ref[:, o : o + NB]), inv, NT)
        px_ref[:, o : o + NB] = xf
        if b == n - 1:
            return
        near, far = slice(o + NB, o + 2 * NB), slice(o + 2 * NB, BS)
        xf = split(xf)
        X1 = split(c_ref[near, o : o + NB])
        x_ref[:, near] = x_ref[:, near] - dot3(xf, X1, NT)
        if b < n - 2:
            X2 = dot3(split(a_ref[far, o : o + NB]), inv, NT)
            c_ref[far, o : o + NB] = X2
            X2 = split(X2)
            a_ref[far, near] = a_ref[far, near] - dot3(X2, X1, NT)
            a_ref[far, far] = a_ref[far, far] - dot3(X2, X2, NT)
            x_ref[:, far] = x_ref[:, far] - dot3(xf, X2, NT)

    T = [a_ref[8 * g : 8 * g + 8, 0:NB] for g in range(NB // 8)]
    left = None
    for b in range(n):
        o = b * NB
        out = eliminate(T)
        if left is not None:
            rest_of(*left)
        for g in range(NB // 8):
            i_ref[b, 8 * g : 8 * g + 8, :] = out[g]
        inv = split(i_ref[b])
        if b < n - 1:
            near = slice(o + NB, o + 2 * NB)
            X1 = dot3(split(a_ref[near, o : o + NB]), inv, NT)
            c_ref[near, o : o + NB] = X1
            X1 = split(X1)
            diagonal = a_ref[near, near] - dot3(X1, X1, NT)
            T = [diagonal[8 * g : 8 * g + 8, :] for g in range(NB // 8)]
        left = (b, o, inv)
    rest_of(*left)
    panel = px_ref[0:16, :]
    grow = rank * 16 + lax.broadcasted_iota(jnp.int32, (16, BS), 0)
    gcol = lax.broadcasted_iota(jnp.int32, (16, BS), 1)
    panel = jnp.where((is_corner == 1) & (gcol > grow), 0.0, panel)
    p_ref[...] = panel
    ws = [None] * n
    wv = [None] * n
    for b in reversed(range(n)):
        o = b * NB
        acc = px_ref[16:, o : o + NB]
        for i in range(b + 1, n):
            acc = acc - dot3(ws[i], split(c_ref[i * NB : (i + 1) * NB, o : o + NB]), NN)
        wv[b] = dot3(split(acc), split(i_ref[b]), NN)
        ws[b] = split(wv[b])
    for half in range(NC):

        @pl.when(core == half)
        def _():
            for q in range(2):
                w_ref[:, q * NB : (q + 1) * NB] = wv[2 * half + q]


def update_kernel(s_ref, w_ref, own_ref, r0_ref, r1_ref, r2_ref, rest_ref, mine_ref, other_ref):
    core = s_ref[CORE]
    for e, recv_ref in enumerate((r0_ref, r1_ref, r2_ref)):
        own = s_ref[OWN + e]
        cols = slice(e * BS, (e + 1) * BS)
        got = jnp.where(own == 1, own_ref[...], recv_ref[...])
        part = dot3(split(w_ref[16 * e : 16 * e + 16, :]), split(got), NT)
        part = rest_ref[:, cols] - part
        low, high = part[0:8, :], part[8:16, :]
        mine_ref[:, cols] = jnp.where(core == 0, low, high)
        other_ref[:, cols] = jnp.where(core == 0, high, low)


def finish_kernel(s_ref, panel_ref, mine_ref, other_ref, out_ref):
    core = s_ref[CORE]
    row = s_ref[RANK] * 16 + core * 8 + lax.broadcasted_iota(jnp.int32, (8, BS), 0)
    col = lax.broadcasted_iota(jnp.int32, (8, BS), 1)
    panel = jnp.where(core == 0, panel_ref[0:8, :], panel_ref[8:16, :])
    values = []
    for e in range(3):
        cols = slice(e * BS, (e + 1) * BS)
        value = (mine_ref[:, cols] + other_ref[:, cols]) * (1.0 / TOKENS)
        on_diagonal = s_ref[ROW_I + 1 + e] == s_ref[COL_J + e]
        values.append(value + jnp.where(on_diagonal & (row == col), DAMPING, 0.0))
    for slot in range(4):
        out = jnp.where(s_ref[PANEL_SLOT] == slot, panel, 0.0)
        for e in range(3):
            out = jnp.where((s_ref[SLOT + e] == slot) & (s_ref[LIVE + e] == 1), values[e], out)
        out_ref[:, slot * BS : (slot + 1) * BS] = out


def vmem(count):
    return [pl.BlockSpec(memory_space=pltpu.VMEM)] * count


SMEM = pl.BlockSpec(memory_space=pltpu.SMEM)


def params(limit=VMEM_LIMIT):
    return pltpu.CompilerParams(vmem_limit_bytes=limit)


def dp_index(z, y, c):
    return (z * NY + y) * NC + c


Z_GROUPS = [[dp_index(z, y, c) for z in range(NZ)] for y in range(NY) for c in range(NC)]
Y_GROUPS = [[dp_index(z, y, c) for y in range(NY)] for z in range(NZ) for c in range(NC)]
CORE_SWAP = [(dp_index(z, y, c), dp_index(z, y, 1 - c)) for z in range(NZ) for y in range(NY) for c in range(NC)]


def exchange(x, groups):
    return lax.all_to_all(x, "dp", 0, 0, axis_index_groups=groups)


def body(act):
    tok = act.shape[0]
    group = lax.axis_index("dp")
    place = lax.dynamic_index_in_dim(
        jnp.asarray(device_table()), group * NBLK + lax.axis_index("blk"), 0, keepdims=False
    )

    piece = jax.ShapeDtypeStruct((NZ, 72, HALF), F32)
    mine, other = pl.pallas_call(
        first_column_kernel,
        out_shape=[piece, piece],
        grid_spec=pltpu.PrefetchScalarGridSpec(
            num_scalar_prefetch=1,
            grid=(1,),
            in_specs=[
                pl.BlockSpec((tok, BS), lambda g, s: (0, 0)),
                pl.BlockSpec((tok, BS), lambda g, s: (0, s[HELD_AT])),
            ],
            out_specs=[pl.BlockSpec((NZ, 72, HALF), lambda g, s: (0, 0, 0))] * 2,
            scratch_shapes=[pltpu.VMEM((BS, BS), F32)],
        ),
        compiler_params=params(),
        name="first_column",
    )(place, act, act)
    first = mine + lax.ppermute(other, "dp", CORE_SWAP)
    over_z = exchange(first, Z_GROUPS)

    both = pl.pallas_call(
        trailing_kernel,
        out_shape=jax.ShapeDtypeStruct((BS, 3 * BS), F32),
        grid_spec=pltpu.PrefetchScalarGridSpec(
            num_scalar_prefetch=1,
            grid=(3,),
            in_specs=[
                pl.BlockSpec((tok, BS), lambda e, s: (0, s[ROW_I + 1 + e])),
                pl.BlockSpec((tok, BS), lambda e, s: (0, s[COL_J + e])),
                HBM,
            ],
            out_specs=pl.BlockSpec((BS, BS), lambda e, s: (0, e)),
        ),
        compiler_params=params(GRAM_LIMIT),
        cost_estimate=pl.CostEstimate(flops=4_000_000_000, bytes_accessed=7_000_000, transcendentals=0),
        name="trailing_gram",
    )(place, act, act, first)
    spread, ready = pl.pallas_call(
        sum_z_kernel,
        out_shape=[jax.ShapeDtypeStruct((NY, 72, HALF), F32), jax.ShapeDtypeStruct((8, NB), F32)],
        in_specs=vmem(1),
        out_specs=vmem(2),
        compiler_params=params(),
        name="sum_over_z",
    )(over_z)
    both = after(both, ready, vmem(1)[0])
    rest_z = lax.psum_scatter(both, "dp", scatter_dimension=0, tiled=True, axis_index_groups=Z_GROUPS)
    rest = lax.psum_scatter(rest_z, "dp", scatter_dimension=0, tiled=True, axis_index_groups=Y_GROUPS)
    over_y = exchange(spread, Y_GROUPS)
    corner_rows, held_rows, own_rows = pl.pallas_call(
        sum_y_kernel,
        out_shape=[
            jax.ShapeDtypeStruct((NZ, 8, HALF), F32),
            jax.ShapeDtypeStruct((NZ, 64, HALF), F32),
            jax.ShapeDtypeStruct((16, HALF), F32),
        ],
        in_specs=[SMEM] + vmem(1),
        out_specs=vmem(3),
        compiler_params=params(),
        name="sum_over_y",
    )(place, over_y)

    corner_rows = exchange(corner_rows, Z_GROUPS)
    column = exchange(held_rows, Z_GROUPS).reshape(BS, HALF)
    share = jnp.concatenate([corner_rows.reshape(64, HALF), own_rows], axis=0)
    share = lax.all_to_all(jnp.broadcast_to(share, (NBLK, 80, HALF)), "blk", 0, 0)
    share_other = lax.ppermute(share, "dp", CORE_SWAP)
    brought = [lax.ppermute(column, "blk", list(pairs)) for pairs in ROUNDS]

    panel, w = pl.pallas_call(
        corner_kernel,
        out_shape=[jax.ShapeDtypeStruct((16, BS), F32), jax.ShapeDtypeStruct((48, HALF), F32)],
        in_specs=[SMEM] + vmem(2),
        out_specs=vmem(2),
        scratch_shapes=[
            pltpu.VMEM((BS, BS), F32),
            pltpu.VMEM((BS, BS), F32),
            pltpu.VMEM((BS // NB, NB, NB), F32),
            pltpu.VMEM((64, BS), F32),
            pltpu.VMEM((64, BS), F32),
        ],
        compiler_params=params(),
        cost_estimate=pl.CostEstimate(flops=CORNER_FLOPS, bytes_accessed=2_000_000, transcendentals=0),
        name="corner",
    )(place, share, share_other)

    part = jax.ShapeDtypeStruct((8, 3 * BS), F32)
    mine, other = pl.pallas_call(
        update_kernel,
        out_shape=[part, part],
        in_specs=[SMEM] + vmem(6),
        out_specs=vmem(2),
        compiler_params=params(),
        name="update",
    )(place, w, column, *brought, rest)
    return pl.pallas_call(
        finish_kernel,
        out_shape=jax.ShapeDtypeStruct((8, 4 * BS), F32),
        in_specs=[SMEM] + vmem(3),
        out_specs=vmem(1)[0],
        compiler_params=params(),
        name="finish",
    )(place, panel, mine, lax.ppermute(other, "dp", CORE_SWAP))


def solution(mesh):
    return jax.shard_map(body, mesh=mesh, in_specs=(P("dp", None),), out_specs=P("dp", "blk"), check_vma=False)
```
